512 devices in a mesh: band: 8 (over y, x_lo), dom: 64 (over x_hi, z, core).
Axes of the slice: x: 4 (x_hi: 2, x_lo: 2; x = x_hi * 2 + x_lo), y: 4, z: 16, core: 2. Of those that a mesh axis runs over, the one named last changes fastest.
Arguments:
- orbitals: bfloat16 [512, 128, 32, 128], P('band', 'dom'), may hold values from -270 to 270
- potential: float32 [128, 32, 128], P('dom'), may hold values from 0 to 4
Outputs:
- rotated: bfloat16 [512, 128, 32, 128], P('band', 'dom')
The draws below stay inside these ranges and needn't reach their ends.
All inputs are finite; a program needn't handle non-finite values.
Results may differ from the reference program's by a relative error of at most 0.025.
Values may be sent and summed in bfloat16 or wider, within the bound.
No kernel may reach another device: no remote copies, remote signals or barrier semaphores. Data moves between devices by JAX's collectives and lax.ppermute only.
A program may use at most 64 MiB of HBM per device.

```python
import math
from functools import partial
import jax
import jax.numpy as jnp
from jax import lax

NORB = 512
NY = 32
NZ = 128
NX = 128


def draw_orbitals(key, part):
    key = jax.random.fold_in(key, 11)
    key_noise, key_shared, key_weight, key_scale = jax.random.split(key, 4)
    position = jnp.arange(NX, dtype=jnp.float32) / max(NX - 1, 1)
    noise = jax.random.truncated_normal(key_noise, -5.0, 5.0, (NORB, NX, NY, NZ), jnp.float32)
    shared = jax.random.truncated_normal(key_shared, -5.0, 5.0, (1, NX, NY, NZ), jnp.float32)
    envelope = 1.0 + 2.0 * position
    weights = jax.random.uniform(key_weight, (NORB, 1, 1, 1), jnp.float32, 0.3, 0.8)
    scales = jnp.exp(jax.random.uniform(key_scale, (NORB, 1, 1, 1), jnp.float32, 0.0, math.log(10.0)))
    return (scales * envelope[None, :, None, None] * (noise + weights * shared)).astype(jnp.bfloat16)


def block_levels(stream_key, extent, cuts, least, largest):
    factor_of, own = 1.0, jax.random.fold_in(stream_key, 6)
    for dim, shards_of in cuts:
        heights = jnp.exp(jax.random.uniform(jax.random.fold_in(own, dim), (shards_of,), jnp.float32, least / len(cuts), largest / len(cuts)))
        factor_of = factor_of * jnp.repeat(heights, extent[dim] // shards_of).reshape([-1 if axis == dim else 1 for axis in range(len(extent))])
    return factor_of


def setup_inputs(seed: int = 0) -> dict:
    key_of = jax.random.split(jax.random.key(seed), 3)
    return {
        "orbitals": draw_orbitals(jax.random.fold_in(key_of[2], 71), 0),
        "potential": jnp.clip(4.0 * jax.random.uniform(key_of[1], (NX, NY, NZ), jnp.float32) ** block_levels(key_of[1], (NX, NY, NZ), ((0, 64),), -0.2, 0.2), 0.0, 4.0),
    }


spectrum_center = 7.5
spectrum_half = 4.5

def neighbours(padded, axis_dim, offset):
    index_list = [slice(None), slice(2, -2), slice(2, -2), slice(2, -2)]
    index_list[axis_dim] = slice(2 + offset, padded.shape[axis_dim] - 2 + offset)
    return padded[tuple(index_list)]

def hamiltonian(padded, potential):
    center = neighbours(padded, 1, 0)
    laplace = -7.5 * center
    for axis_dim in (1, 2, 3):
        near_sum = neighbours(padded, axis_dim, 1) + neighbours(padded, axis_dim, -1)
        far_sum = neighbours(padded, axis_dim, 2) + neighbours(padded, axis_dim, -2)
        laplace = laplace + 4.0 / 3.0 * near_sum - 1.0 / 12.0 * far_sum
    return (-0.5 * laplace + potential * center, center)

def chebyshev(field, operate):
    image, anchor = operate(field)
    degree_one = ((image - spectrum_center * anchor) / spectrum_half).astype(jnp.bfloat16)
    image, current = operate(degree_one)
    second = (2.0 * (image - spectrum_center * current) / spectrum_half - anchor).astype(jnp.bfloat16)
    image, latest = operate(second)
    return (2.0 * (image - spectrum_center * latest) / spectrum_half - current).astype(jnp.bfloat16)

def local_operator(field, potential):
    padded = jnp.pad(field.astype(jnp.float32), ((0, 0), (2, 2), (2, 2), (2, 2)))
    return hamiltonian(padded, potential)

def reference(orbitals, potential):
    grouped = orbitals.reshape(NORB // 8, 8, NX, NY, NZ)
    operate = partial(local_operator, potential=potential)
    filtered = lax.map(lambda orbital_group: chebyshev(orbital_group, operate), grouped)
    flat = filtered.reshape(NORB, NX * NY * NZ)
    gram = lax.dot_general(flat.astype(jnp.float32), flat.astype(jnp.float32), (((1,), (1,)), ((), ())), preferred_element_type=jnp.float32) / (NX * NY * NZ)
    factor = jnp.linalg.cholesky(gram)
    inverse_factor = lax.linalg.triangular_solve(factor, jnp.eye(NORB, dtype=jnp.float32), left_side=True, lower=True)
    rotation = inverse_factor.astype(jnp.bfloat16)
    rotated = jnp.dot(rotation.astype(jnp.float32), flat.astype(jnp.float32), preferred_element_type=jnp.float32).astype(jnp.bfloat16)
    return rotated.reshape(NORB, NX, NY, NZ)
```

```python
from functools import partial

import jax
import jax.numpy as jnp
from jax import lax
from jax.sharding import PartitionSpec as P

spectrum_center = 7.5
spectrum_half = 4.5


def padded_2(cells, sides, width):
    for axis, dim in sides:
        count = lax.axis_size(axis)
        ends = count - 1
        head = lax.slice_in_dim(cells, 0, width, axis=dim)
        tail = lax.slice_in_dim(cells, cells.shape[dim] - width, cells.shape[dim], axis=dim)
        cells = jnp.concatenate(
            [
                lax.ppermute(tail, axis, [(i, (i + 1) % count) for i in range(ends)]),
                cells,
                lax.ppermute(head, axis, [((i + 1) % count, i) for i in range(ends)]),
            ],
            axis=dim,
        )
    return cells


def neighbours(padded, axis_dim, offset):
    index_list = [slice(None), slice(2, -2), slice(2, -2), slice(2, -2)]
    index_list[axis_dim] = slice(2 + offset, padded.shape[axis_dim] - 2 + offset)
    return padded[tuple(index_list)]


def hamiltonian(padded, potential):
    center = neighbours(padded, 1, 0)
    laplace = -7.5 * center
    for axis_dim in (1, 2, 3):
        near_sum = neighbours(padded, axis_dim, 1) + neighbours(padded, axis_dim, -1)
        far_sum = neighbours(padded, axis_dim, 2) + neighbours(padded, axis_dim, -2)
        laplace = laplace + 4.0 / 3.0 * near_sum - 1.0 / 12.0 * far_sum
    return (-0.5 * laplace + potential * center, center)


def chebyshev(field, operate):
    image, anchor = operate(field)
    degree_one = ((image - spectrum_center * anchor) / spectrum_half).astype(jnp.bfloat16)
    image, current = operate(degree_one)
    second = (2.0 * (image - spectrum_center * current) / spectrum_half - anchor).astype(
        jnp.bfloat16
    )
    image, latest = operate(second)
    return (2.0 * (image - spectrum_center * latest) / spectrum_half - current).astype(jnp.bfloat16)


def operator_on(field, potential):
    widened = padded_2(field, (("dom", 1),), 2)
    padded = jnp.pad(widened.astype(jnp.float32), ((0, 0), (0, 0), (2, 2), (2, 2)))
    return hamiltonian(padded, potential)


def rotation_from(gram):
    factor = jnp.linalg.cholesky(gram)
    identity = jnp.eye(gram.shape[0], dtype=jnp.float32)
    inverse_factor = lax.linalg.triangular_solve(factor, identity, left_side=True, lower=True)
    return inverse_factor.astype(jnp.bfloat16)


def exchange(pieces, axis):
    return lax.all_to_all(pieces, axis, 0, 0, tiled=True)


def summed_everywhere(terms):
    bands, doms = lax.axis_size("band"), lax.axis_size("dom")
    count = terms.shape[0]
    rows = jnp.sum(exchange(terms.reshape(bands, count // bands, count), "band"), axis=0)
    one = rows.reshape(doms, count // (bands * doms), count)
    one = jnp.sum(exchange(one, "dom"), axis=0, keepdims=True)
    rows = exchange(jnp.broadcast_to(one, (doms,) + one.shape[1:]), "dom")
    rows = rows.reshape(1, count // bands, count)
    return exchange(jnp.broadcast_to(rows, (bands,) + rows.shape[1:]), "band").reshape(count, count)


def local(orbitals, potential):
    orb_count = orbitals.shape[0]
    bands = lax.axis_size("band")
    cells_dev = orbitals.shape[1] * orbitals.shape[2] * orbitals.shape[3]
    total_cells = cells_dev * lax.axis_size("dom")
    filtered = chebyshev(orbitals, partial(operator_on, potential=potential))
    flat = filtered.reshape(orb_count, cells_dev)
    everyone = lax.all_to_all(flat, "band", 1, 0, tiled=True)
    contract = (((1,), (1,)), ((), ()))
    terms = lax.dot_general(everyone, everyone, contract, preferred_element_type=jnp.float32)
    gram = summed_everywhere(terms) / total_cells
    rotation = rotation_from(gram)
    turned = jnp.dot(rotation, everyone, preferred_element_type=jnp.float32).astype(jnp.bfloat16)
    result = lax.all_to_all(turned, "band", 0, 1, tiled=True)
    return result.reshape(orbitals.shape)


def solution(mesh):
    placed = (P("band", "dom", None, None), P("dom", None, None))
    return jax.shard_map(
        local, mesh=mesh, in_specs=placed, out_specs=P("band", "dom", None, None), check_vma=False
    )
```

```python
from functools import partial

import jax
import jax.numpy as jnp
from jax import lax
from jax.experimental import pallas as pl
from jax.experimental.pallas import tpu as pltpu
from jax.sharding import PartitionSpec as P

HIGHEST = lax.Precision.HIGHEST

spectrum_center = 7.5
spectrum_half = 4.5


def padded_2(cells, sides, width):
    for axis, dim in sides:
        count = lax.axis_size(axis)
        ends = count - 1
        head = lax.slice_in_dim(cells, 0, width, axis=dim)
        tail = lax.slice_in_dim(cells, cells.shape[dim] - width, cells.shape[dim], axis=dim)
        cells = jnp.concatenate(
            [
                lax.ppermute(tail, axis, [(i, (i + 1) % count) for i in range(ends)]),
                cells,
                lax.ppermute(head, axis, [((i + 1) % count, i) for i in range(ends)]),
            ],
            axis=dim,
        )
    return cells


def neighbours(padded, axis_dim, offset):
    index_list = [slice(None), slice(2, -2), slice(2, -2), slice(2, -2)]
    index_list[axis_dim] = slice(2 + offset, padded.shape[axis_dim] - 2 + offset)
    return padded[tuple(index_list)]


def hamiltonian(padded, potential):
    center = neighbours(padded, 1, 0)
    laplace = -7.5 * center
    for axis_dim in (1, 2, 3):
        near_sum = neighbours(padded, axis_dim, 1) + neighbours(padded, axis_dim, -1)
        far_sum = neighbours(padded, axis_dim, 2) + neighbours(padded, axis_dim, -2)
        laplace = laplace + 4.0 / 3.0 * near_sum - 1.0 / 12.0 * far_sum
    return (-0.5 * laplace + potential * center, center)


def chebyshev(field, operate):
    image, anchor = operate(field)
    degree_one = ((image - spectrum_center * anchor) / spectrum_half).astype(jnp.bfloat16)
    image, current = operate(degree_one)
    second = (2.0 * (image - spectrum_center * current) / spectrum_half - anchor).astype(
        jnp.bfloat16
    )
    image, latest = operate(second)
    return (2.0 * (image - spectrum_center * latest) / spectrum_half - current).astype(jnp.bfloat16)


def operator_on(field, potential):
    widened = padded_2(field, (("dom", 1),), 2)
    padded = jnp.pad(widened.astype(jnp.float32), ((0, 0), (0, 0), (2, 2), (2, 2)))
    return hamiltonian(padded, potential)


def dot_nn(a, b):
    return lax.dot_general(a, b, (((1,), (0,)), ((), ())), precision=HIGHEST, preferred_element_type=jnp.float32)


def dot_nt(a, b):
    return lax.dot_general(a, b, (((1,), (1,)), ((), ())), precision=HIGHEST, preferred_element_type=jnp.float32)


def reciprocal(value):
    guess = pl.reciprocal(value, approx=True)
    return guess * (2.0 - value * guess)


def inverse_factor_of_block(rows):
    lane = lax.broadcasted_iota(jnp.int32, (8, 128), 1)
    sub = lax.broadcasted_iota(jnp.int32, (8, 128), 0)
    rows = list(rows)
    out = []
    for p in range(16):
        k0 = 8 * p
        inside = (lane >= k0) & (lane < k0 + 8)
        x = rows[p]
        columns = [jnp.broadcast_to(x[:, k0 + j : k0 + j + 1], (8, 128)) for j in range(8)]
        a = [[jnp.broadcast_to(columns[j][i : i + 1, :], (8, 128)) for j in range(i + 1)] for i in range(8)]
        x = jnp.where(inside, (lane - k0 == sub).astype(jnp.float32), x)
        z = [jnp.broadcast_to(x[i : i + 1, :], (8, 128)) for i in range(8)]
        inv, m = [], [[None] * 8 for _ in range(8)]
        for j in range(8):
            inv.append(reciprocal(a[j][j]))
            for l in range(j + 1, 8):
                m[l][j] = a[l][j] * inv[j]
            for l in range(j + 1, 8):
                for q in range(j + 1, l + 1):
                    a[l][q] = a[l][q] - m[l][j] * a[q][j]
                z[l] = z[l] - m[l][j] * z[j]
        w = z[0] * lax.rsqrt(a[0][0])
        for i in range(1, 8):
            w = jnp.where(sub == i, z[i] * lax.rsqrt(a[i][i]), w)
        out.append(jnp.where(lane < k0 + 8, w, 0.0))
        if p == 15:
            break
        y = [z[j] * inv[j] for j in range(8)]
        for l in range(7, 0, -1):
            for j in range(l):
                y[j] = y[j] - m[l][j] * y[l]
        for i in range(p + 1, 16):
            c = [jnp.broadcast_to(rows[i][:, k0 + j : k0 + j + 1], (8, 128)) for j in range(8)]
            t = [c[j] * y[j] for j in range(8)]
            t = ((t[0] + t[1]) + (t[2] + t[3])) + ((t[4] + t[5]) + (t[6] + t[7]))
            rows[i] = jnp.where(inside, 0.0, rows[i]) - t
    return out


def rotation_kernel(gram_ref, out_ref, s_ref, a_ref, w_ref):
    n, b = gram_ref.shape[0], 128
    blocks = n // b
    s_ref[...] = gram_ref[...]
    a_ref[...] = jnp.zeros_like(a_ref)
    for k in range(blocks):
        lo, hi = k * b, (k + 1) * b
        out = inverse_factor_of_block([s_ref[lo + 8 * i : lo + 8 * i + 8, lo:hi] for i in range(16)])
        for i in range(16):
            w_ref[8 * i : 8 * i + 8, :] = out[i]
        w = w_ref[...]
        out_ref[lo:hi, lo:hi] = w.astype(jnp.bfloat16)
        if hi < n:
            out_ref[lo:hi, hi:] = jnp.zeros((b, n - hi), jnp.bfloat16)
            upper = dot_nn(w, s_ref[lo:hi, hi:])
            lower = dot_nt(s_ref[hi:, lo:hi], w)
            s_ref[hi:, hi:] -= dot_nn(lower, upper)
        if k > 0:
            v = dot_nn(w, a_ref[lo:hi, :lo])
            out_ref[lo:hi, :lo] = v.astype(jnp.bfloat16)
            if hi < n:
                a_ref[hi:, :lo] -= dot_nn(lower, v)
        if hi < n:
            a_ref[hi:, lo:hi] = -dot_nn(lower, w)


def rotation_from(gram):
    n = gram.shape[0]
    return pl.pallas_call(
        rotation_kernel,
        out_shape=jax.ShapeDtypeStruct((n, n), jnp.bfloat16),
        in_specs=[pl.BlockSpec(memory_space=pltpu.VMEM)],
        out_specs=pl.BlockSpec(memory_space=pltpu.VMEM),
        scratch_shapes=[
            pltpu.VMEM((n, n), jnp.float32),
            pltpu.VMEM((n, n), jnp.float32),
            pltpu.VMEM((128, 128), jnp.float32),
        ],
        compiler_params=pltpu.CompilerParams(vmem_limit_bytes=32 * 1024 * 1024),
    )(gram)


def exchange(pieces, axis):
    return lax.all_to_all(pieces, axis, 0, 0, tiled=True)


def summed_everywhere(terms):
    bands, doms = lax.axis_size("band"), lax.axis_size("dom")
    count = terms.shape[0]
    rows = jnp.sum(exchange(terms.reshape(bands, count // bands, count), "band"), axis=0)
    one = rows.reshape(doms, count // (bands * doms), count)
    one = jnp.sum(exchange(one, "dom"), axis=0, keepdims=True)
    rows = exchange(jnp.broadcast_to(one, (doms,) + one.shape[1:]), "dom")
    rows = rows.reshape(1, count // bands, count)
    return exchange(jnp.broadcast_to(rows, (bands,) + rows.shape[1:]), "band").reshape(count, count)


def local(orbitals, potential):
    orb_count = orbitals.shape[0]
    bands = lax.axis_size("band")
    cells_dev = orbitals.shape[1] * orbitals.shape[2] * orbitals.shape[3]
    total_cells = cells_dev * lax.axis_size("dom")
    filtered = chebyshev(orbitals, partial(operator_on, potential=potential))
    flat = filtered.reshape(orb_count, cells_dev)
    everyone = lax.all_to_all(flat, "band", 1, 0, tiled=True)
    contract = (((1,), (1,)), ((), ()))
    terms = lax.dot_general(everyone, everyone, contract, preferred_element_type=jnp.float32)
    gram = summed_everywhere(terms) / total_cells
    rotation = rotation_from(gram)
    turned = jnp.dot(rotation, everyone, preferred_element_type=jnp.float32).astype(jnp.bfloat16)
    result = lax.all_to_all(turned, "band", 0, 1, tiled=True)
    return result.reshape(orbitals.shape)


def solution(mesh):
    placed = (P("band", "dom", None, None), P("dom", None, None))
    return jax.shard_map(
        local, mesh=mesh, in_specs=placed, out_specs=P("band", "dom", None, None), check_vma=False
    )
```

```python
from functools import partial

import jax
import jax.numpy as jnp
from jax import lax
from jax.experimental import pallas as pl
from jax.experimental.pallas import tpu as pltpu
from jax.sharding import Mesh
from jax.sharding import PartitionSpec as P

BAND, DOM = ("y", "x_lo"), ("x_hi", "z", "core")
NEAR, FAR = ("y", "x_lo", "core"), ("x_hi", "z")

HIGHEST = lax.Precision.HIGHEST

spectrum_center = 7.5
spectrum_half = 4.5


def padded_2(cells, sides, width):
    for axis, dim in sides:
        count = lax.axis_size(axis)
        ends = count - 1
        head = lax.slice_in_dim(cells, 0, width, axis=dim)
        tail = lax.slice_in_dim(cells, cells.shape[dim] - width, cells.shape[dim], axis=dim)
        cells = jnp.concatenate(
            [
                lax.ppermute(tail, axis, [(i, (i + 1) % count) for i in range(ends)]),
                cells,
                lax.ppermute(head, axis, [((i + 1) % count, i) for i in range(ends)]),
            ],
            axis=dim,
        )
    return cells


def neighbours(padded, axis_dim, offset):
    index_list = [slice(None), slice(2, -2), slice(2, -2), slice(2, -2)]
    index_list[axis_dim] = slice(2 + offset, padded.shape[axis_dim] - 2 + offset)
    return padded[tuple(index_list)]


def hamiltonian(padded, potential):
    center = neighbours(padded, 1, 0)
    laplace = -7.5 * center
    for axis_dim in (1, 2, 3):
        near_sum = neighbours(padded, axis_dim, 1) + neighbours(padded, axis_dim, -1)
        far_sum = neighbours(padded, axis_dim, 2) + neighbours(padded, axis_dim, -2)
        laplace = laplace + 4.0 / 3.0 * near_sum - 1.0 / 12.0 * far_sum
    return (-0.5 * laplace + potential * center, center)


def chebyshev(field, operate):
    image, anchor = operate(field)
    degree_one = ((image - spectrum_center * anchor) / spectrum_half).astype(jnp.bfloat16)
    image, current = operate(degree_one)
    second = (2.0 * (image - spectrum_center * current) / spectrum_half - anchor).astype(
        jnp.bfloat16
    )
    image, latest = operate(second)
    return (2.0 * (image - spectrum_center * latest) / spectrum_half - current).astype(jnp.bfloat16)


def operator_on(field, potential):
    widened = padded_2(field, ((DOM, 1),), 2)
    padded = jnp.pad(widened.astype(jnp.float32), ((0, 0), (0, 0), (2, 2), (2, 2)))
    return hamiltonian(padded, potential)


def dot_nn(a, b):
    return lax.dot_general(a, b, (((1,), (0,)), ((), ())), precision=HIGHEST, preferred_element_type=jnp.float32)


def dot_nt(a, b):
    return lax.dot_general(a, b, (((1,), (1,)), ((), ())), precision=HIGHEST, preferred_element_type=jnp.float32)


def reciprocal(value):
    guess = pl.reciprocal(value, approx=True)
    return guess * (2.0 - value * guess)


def inverse_factor_of_block(rows):
    lane = lax.broadcasted_iota(jnp.int32, (8, 128), 1)
    sub = lax.broadcasted_iota(jnp.int32, (8, 128), 0)
    rows = list(rows)
    out = []
    for p in range(16):
        k0 = 8 * p
        inside = (lane >= k0) & (lane < k0 + 8)
        x = rows[p]
        columns = [jnp.broadcast_to(x[:, k0 + j : k0 + j + 1], (8, 128)) for j in range(8)]
        a = [[jnp.broadcast_to(columns[j][i : i + 1, :], (8, 128)) for j in range(i + 1)] for i in range(8)]
        x = jnp.where(inside, (lane - k0 == sub).astype(jnp.float32), x)
        z = [jnp.broadcast_to(x[i : i + 1, :], (8, 128)) for i in range(8)]
        inv, m = [], [[None] * 8 for _ in range(8)]
        for j in range(8):
            inv.append(reciprocal(a[j][j]))
            for l in range(j + 1, 8):
                m[l][j] = a[l][j] * inv[j]
            for l in range(j + 1, 8):
                for q in range(j + 1, l + 1):
                    a[l][q] = a[l][q] - m[l][j] * a[q][j]
                z[l] = z[l] - m[l][j] * z[j]
        w = z[0] * lax.rsqrt(a[0][0])
        for i in range(1, 8):
            w = jnp.where(sub == i, z[i] * lax.rsqrt(a[i][i]), w)
        out.append(jnp.where(lane < k0 + 8, w, 0.0))
        if p == 15:
            break
        y = [z[j] * inv[j] for j in range(8)]
        for l in range(7, 0, -1):
            for j in range(l):
                y[j] = y[j] - m[l][j] * y[l]
        for i in range(p + 1, 16):
            c = [jnp.broadcast_to(rows[i][:, k0 + j : k0 + j + 1], (8, 128)) for j in range(8)]
            t = [c[j] * y[j] for j in range(8)]
            t = ((t[0] + t[1]) + (t[2] + t[3])) + ((t[4] + t[5]) + (t[6] + t[7]))
            rows[i] = jnp.where(inside, 0.0, rows[i]) - t
    return out


def gram_kernel(field_ref, tiles_ref):
    tile = 0
    for i in range(field_ref.shape[0] // 128):
        rows = slice(128 * i, 128 * i + 128)
        terms = lax.dot_general(
            field_ref[rows, :],
            field_ref[: 128 * i + 128, :],
            (((1,), (1,)), ((), ())),
            preferred_element_type=jnp.float32,
        )
        for j in range(i + 1):
            tiles_ref[128 * tile : 128 * tile + 128, :] = terms[:, 128 * j : 128 * j + 128]
            tile += 1


def gram_tiles(field):
    count = field.shape[0] // 128
    return pl.pallas_call(
        gram_kernel,
        out_shape=jax.ShapeDtypeStruct((64 * count * (count + 1), 128), jnp.float32),
        in_specs=[pl.BlockSpec(memory_space=pltpu.VMEM)],
        out_specs=pl.BlockSpec(memory_space=pltpu.VMEM),
        compiler_params=pltpu.CompilerParams(vmem_limit_bytes=32 * 1024 * 1024),
    )(field)


def rotation_kernel(tiles_ref, field_ref, out_ref, s_ref, a_ref, w_ref, r_ref):
    n, b = field_ref.shape[0], 128
    tile = 0
    for i in range(n // b):
        for j in range(i + 1):
            s_ref[b * i : b * i + b, b * j : b * j + b] = tiles_ref[b * tile : b * tile + b, :]
            tile += 1
    for k in range(n // b):
        lo, hi = k * b, (k + 1) * b
        out = inverse_factor_of_block([s_ref[lo + 8 * i : lo + 8 * i + 8, lo:hi] for i in range(16)])
        for i in range(16):
            w_ref[8 * i : 8 * i + 8, :] = out[i]
        w = w_ref[...]
        r_ref[lo:hi, lo:hi] = w.astype(jnp.bfloat16)
        if hi < n:
            lower = dot_nt(s_ref[hi:, lo:hi], w)
            s_ref[hi:, hi:] -= dot_nt(lower, lower)
        if k > 0:
            v = dot_nn(w, a_ref[lo:hi, :lo])
            r_ref[lo:hi, :lo] = v.astype(jnp.bfloat16)
            if hi < n:
                a_ref[hi:, :lo] -= dot_nn(lower, v)
        if hi < n:
            a_ref[hi:, lo:hi] = -dot_nn(lower, w)
        turned = jnp.dot(r_ref[lo:hi, :hi], field_ref[:hi, :], preferred_element_type=jnp.float32)
        out_ref[lo:hi, :] = turned.astype(jnp.bfloat16)


def rotated_by(tiles, field):
    n = field.shape[0]
    return pl.pallas_call(
        rotation_kernel,
        out_shape=jax.ShapeDtypeStruct(field.shape, jnp.bfloat16),
        in_specs=[pl.BlockSpec(memory_space=pltpu.VMEM)] * 2,
        out_specs=pl.BlockSpec(memory_space=pltpu.VMEM),
        scratch_shapes=[
            pltpu.VMEM((n, n), jnp.float32),
            pltpu.VMEM((n, n), jnp.float32),
            pltpu.VMEM((128, 128), jnp.float32),
            pltpu.VMEM((n, n), jnp.bfloat16),
        ],
        compiler_params=pltpu.CompilerParams(vmem_limit_bytes=32 * 1024 * 1024),
    )(tiles, field)


def exchange(pieces, axis):
    return lax.all_to_all(pieces, axis, 0, 0, tiled=True)


def summed_everywhere(terms, scale):
    first, second = lax.axis_size(NEAR), lax.axis_size(FAR)
    rows = terms.shape[0] // first
    share = -(-rows // second)
    part = jnp.sum(exchange(terms.reshape(first, rows, 128), NEAR), axis=0)
    part = jnp.pad(part, ((0, share * second - rows), (0, 0))).reshape(second, share, 128)
    own = jnp.sum(exchange(part, FAR), axis=0, keepdims=True) * scale
    part = exchange(jnp.broadcast_to(own, (second, share, 128)), FAR)
    part = part.reshape(share * second, 128)[:rows]
    return exchange(jnp.broadcast_to(part[None], (first, rows, 128)), NEAR).reshape(terms.shape)


def local(orbitals, potential):
    orb_count = orbitals.shape[0]
    cells_dev = orbitals.shape[1] * orbitals.shape[2] * orbitals.shape[3]
    total_cells = cells_dev * lax.axis_size(DOM)
    filtered = chebyshev(orbitals, partial(operator_on, potential=potential))
    flat = filtered.reshape(orb_count, cells_dev)
    everyone = lax.all_to_all(flat, BAND, 1, 0, tiled=True)
    tiles = summed_everywhere(gram_tiles(everyone), 1.0 / total_cells)
    turned = rotated_by(tiles, everyone)
    result = lax.all_to_all(turned, BAND, 0, 1, tiled=True)
    return result.reshape(orbitals.shape)


def solution(mesh):
    named = Mesh(mesh.devices.reshape(4, 2, 2, 16, 2), ("y", "x_lo", "x_hi", "z", "core"))
    placed = (P(BAND, DOM, None, None), P(DOM, None, None))
    return jax.shard_map(
        local, mesh=named, in_specs=placed, out_specs=P(BAND, DOM, None, None), check_vma=False
    )
```

```python
from functools import partial

import jax
import jax.numpy as jnp
import numpy as np
from jax import lax
from jax.experimental import pallas as pl
from jax.experimental.pallas import tpu as pltpu
from jax.sharding import Mesh
from jax.sharding import PartitionSpec as P

BAND, DOM = ("y", "x_lo"), ("x_hi", "z", "core")
NEAR, FAR = ("y", "x_lo", "core"), ("x_hi", "z")

PARTS = 2

HIGHEST = lax.Precision.HIGHEST

spectrum_center = 7.5
spectrum_half = 4.5


def stencil_matrices():
    def band(count):
        away = np.abs(np.arange(count)[:, None] - np.arange(count)[None, :])
        return 16.0 * (away == 1) - 1.0 * (away == 2)

    eye, none = np.eye(32), np.zeros((32, 32))
    own = np.block([[band(32), 16.0 * eye], [16.0 * eye, band(32)]])
    left = np.block([[-eye, 16.0 * eye], [none, -eye]])
    right = np.block([[-eye, none], [16.0 * eye, -eye]])
    across = [np.kron(np.eye(2), part) for part in (left, own, right)]
    return np.concatenate(across, axis=1), band(128) - 90.0 * np.eye(128)


def stencil_kernel(degree, left_ref, cells_ref, right_ref, potential_ref, across_ref, along_ref, *rest):
    out_ref = rest[-1]
    double = 1.0 if degree == 0 else 2.0
    weight = (potential_ref[...] - spectrum_center) * (double / spectrum_half)
    weight = jnp.concatenate([weight, weight], axis=0)
    for step in range(cells_ref.shape[0] // 128):
        rows = slice(128 * step, 128 * step + 128)
        cells = cells_ref[rows, :]
        stack = jnp.concatenate([left_ref[rows, :], cells, right_ref[rows, :]], axis=0)
        laplace = jnp.dot(across_ref[...], stack, preferred_element_type=jnp.float32)
        laplace += jnp.dot(cells, along_ref[...], preferred_element_type=jnp.float32)
        image = weight * cells.astype(jnp.float32) - laplace * (double / (24.0 * spectrum_half))
        if degree > 0:
            image = image - rest[0][rows, :].astype(jnp.float32)
        out_ref[rows, :] = image.astype(jnp.bfloat16)


def filtered_by_one(degree, sides, cells, before, potential, matrices):
    operands = [sides[0], cells, sides[1], potential, *matrices] + ([before] if degree > 0 else [])
    return pl.pallas_call(
        partial(stencil_kernel, degree),
        out_shape=jax.ShapeDtypeStruct(cells.shape, jnp.bfloat16),
        in_specs=[pl.BlockSpec(memory_space=pltpu.VMEM)] * len(operands),
        out_specs=pl.BlockSpec(memory_space=pltpu.VMEM),
        compiler_params=pltpu.CompilerParams(vmem_limit_bytes=32 * 1024 * 1024),
        cost_estimate=pl.CostEstimate(
            flops=1024 * cells.size, bytes_accessed=10 * cells.size, transcendentals=0
        ),
    )(*operands)


def halo(cells):
    count = lax.axis_size(DOM)
    left = lax.ppermute(cells, DOM, [(i, i + 1) for i in range(count - 1)])
    right = lax.ppermute(cells, DOM, [(i + 1, i) for i in range(count - 1)])
    return left, right


def chebyshev(groups, potential):
    matrices = [jnp.asarray(part, jnp.bfloat16) for part in stencil_matrices()]
    latest, previous = list(groups), [None] * len(groups)
    sides = [halo(cells) for cells in latest]
    for degree in range(3):
        for g in range(len(groups)):
            cells = latest[g]
            latest[g] = filtered_by_one(degree, sides[g], cells, previous[g], potential, matrices)
            previous[g] = cells
            if degree < 2:
                sides[g] = halo(latest[g])
    return latest


def dot_nn(a, b):
    return lax.dot_general(a, b, (((1,), (0,)), ((), ())), precision=HIGHEST, preferred_element_type=jnp.float32)


def dot_nt(a, b):
    return lax.dot_general(a, b, (((1,), (1,)), ((), ())), precision=HIGHEST, preferred_element_type=jnp.float32)


def reciprocal(value):
    guess = pl.reciprocal(value, approx=True)
    return guess * (2.0 - value * guess)


def inverse_factor_of_block(rows):
    lane = lax.broadcasted_iota(jnp.int32, (8, 128), 1)
    sub = lax.broadcasted_iota(jnp.int32, (8, 128), 0)
    rows = list(rows)
    out = []
    for p in range(16):
        k0 = 8 * p
        inside = (lane >= k0) & (lane < k0 + 8)
        x = rows[p]
        columns = [jnp.broadcast_to(x[:, k0 + j : k0 + j + 1], (8, 128)) for j in range(8)]
        a = [[jnp.broadcast_to(columns[j][i : i + 1, :], (8, 128)) for j in range(i + 1)] for i in range(8)]
        x = jnp.where(inside, (lane - k0 == sub).astype(jnp.float32), x)
        z = [jnp.broadcast_to(x[i : i + 1, :], (8, 128)) for i in range(8)]
        inv, m = [], [[None] * 8 for _ in range(8)]
        for j in range(8):
            inv.append(reciprocal(a[j][j]))
            for l in range(j + 1, 8):
                m[l][j] = a[l][j] * inv[j]
            for l in range(j + 1, 8):
                for q in range(j + 1, l + 1):
                    a[l][q] = a[l][q] - m[l][j] * a[q][j]
                z[l] = z[l] - m[l][j] * z[j]
        w = z[0] * lax.rsqrt(a[0][0])
        for i in range(1, 8):
            w = jnp.where(sub == i, z[i] * lax.rsqrt(a[i][i]), w)
        out.append(jnp.where(lane < k0 + 8, w, 0.0))
        if p == 15:
            break
        y = [z[j] * inv[j] for j in range(8)]
        for l in range(7, 0, -1):
            for j in range(l):
                y[j] = y[j] - m[l][j] * y[l]
        for i in range(p + 1, 16):
            c = [jnp.broadcast_to(rows[i][:, k0 + j : k0 + j + 1], (8, 128)) for j in range(8)]
            t = [c[j] * y[j] for j in range(8)]
            t = ((t[0] + t[1]) + (t[2] + t[3])) + ((t[4] + t[5]) + (t[6] + t[7]))
            rows[i] = jnp.where(inside, 0.0, rows[i]) - t
    return out


def gram_kernel(field_ref, tiles_ref):
    tile = 0
    for i in range(field_ref.shape[0] // 128):
        rows = slice(128 * i, 128 * i + 128)
        terms = lax.dot_general(
            field_ref[rows, :],
            field_ref[: 128 * i + 128, :],
            (((1,), (1,)), ((), ())),
            preferred_element_type=jnp.float32,
        )
        for j in range(i + 1):
            tiles_ref[128 * tile : 128 * tile + 128, :] = terms[:, 128 * j : 128 * j + 128]
            tile += 1


def gram_tiles(field):
    count = field.shape[0] // 128
    return pl.pallas_call(
        gram_kernel,
        out_shape=jax.ShapeDtypeStruct((64 * count * (count + 1), 128), jnp.float32),
        in_specs=[pl.BlockSpec(memory_space=pltpu.VMEM)],
        out_specs=pl.BlockSpec(memory_space=pltpu.VMEM),
        compiler_params=pltpu.CompilerParams(vmem_limit_bytes=32 * 1024 * 1024),
    )(field)


def rotation_kernel(tiles_ref, field_ref, out_ref, s_ref, a_ref, w_ref, r_ref):
    n, b = field_ref.shape[0], 128
    tile = 0
    for i in range(n // b):
        for j in range(i + 1):
            s_ref[b * i : b * i + b, b * j : b * j + b] = tiles_ref[b * tile : b * tile + b, :]
            tile += 1
    for k in range(n // b):
        lo, hi = k * b, (k + 1) * b
        out = inverse_factor_of_block([s_ref[lo + 8 * i : lo + 8 * i + 8, lo:hi] for i in range(16)])
        for i in range(16):
            w_ref[8 * i : 8 * i + 8, :] = out[i]
        w = w_ref[...]
        r_ref[lo:hi, lo:hi] = w.astype(jnp.bfloat16)
        if hi < n:
            lower = dot_nt(s_ref[hi:, lo:hi], w)
            s_ref[hi:, hi:] -= dot_nt(lower, lower)
        if k > 0:
            v = dot_nn(w, a_ref[lo:hi, :lo])
            r_ref[lo:hi, :lo] = v.astype(jnp.bfloat16)
            if hi < n:
                a_ref[hi:, :lo] -= dot_nn(lower, v)
        if hi < n:
            a_ref[hi:, lo:hi] = -dot_nn(lower, w)
        turned = jnp.dot(r_ref[lo:hi, :hi], field_ref[:hi, :], preferred_element_type=jnp.float32)
        out_ref[lo:hi, :] = turned.astype(jnp.bfloat16)


def rotated_by(tiles, field):
    n = field.shape[0]
    return pl.pallas_call(
        rotation_kernel,
        out_shape=jax.ShapeDtypeStruct(field.shape, jnp.bfloat16),
        in_specs=[pl.BlockSpec(memory_space=pltpu.VMEM)] * 2,
        out_specs=pl.BlockSpec(memory_space=pltpu.VMEM),
        scratch_shapes=[
            pltpu.VMEM((n, n), jnp.float32),
            pltpu.VMEM((n, n), jnp.float32),
            pltpu.VMEM((128, 128), jnp.float32),
            pltpu.VMEM((n, n), jnp.bfloat16),
        ],
        compiler_params=pltpu.CompilerParams(vmem_limit_bytes=32 * 1024 * 1024),
    )(tiles, field)


def exchange(pieces, axis):
    return lax.all_to_all(pieces, axis, 0, 0, tiled=True)


def summed_everywhere(terms, scale):
    first, second = lax.axis_size(NEAR), lax.axis_size(FAR)
    rows = terms.shape[0] // first
    share = -(-rows // second)
    part = jnp.sum(exchange(terms.reshape(first, rows, 128), NEAR), axis=0)
    part = jnp.pad(part, ((0, share * second - rows), (0, 0))).reshape(second, share, 128)
    own = jnp.sum(exchange(part, FAR), axis=0, keepdims=True) * scale
    part = exchange(jnp.broadcast_to(own, (second, share, 128)), FAR)
    part = part.reshape(share * second, 128)[:rows]
    return exchange(jnp.broadcast_to(part[None], (first, rows, 128)), NEAR).reshape(terms.shape)


def local(orbitals, potential):
    cells_dev = orbitals.shape[1] * orbitals.shape[2] * orbitals.shape[3]
    total_cells = cells_dev * lax.axis_size(DOM)
    slabs = orbitals.reshape(PARTS, -1, orbitals.shape[3])
    filtered = chebyshev([slabs[g] for g in range(PARTS)], potential.reshape(-1, potential.shape[2]))
    flat = jnp.concatenate([part.reshape(-1, cells_dev) for part in filtered], axis=0)
    everyone = lax.all_to_all(flat, BAND, 1, 0, tiled=True)
    tiles = summed_everywhere(gram_tiles(everyone), 1.0 / total_cells)
    turned = rotated_by(tiles, everyone)
    result = lax.all_to_all(turned, BAND, 0, 1, tiled=True)
    return result.reshape(orbitals.shape)


def solution(mesh):
    named = Mesh(mesh.devices.reshape(4, 2, 2, 16, 2), ("y", "x_lo", "x_hi", "z", "core"))
    placed = (P(BAND, DOM, None, None), P(DOM, None, None))
    return jax.shard_map(
        local, mesh=named, in_specs=placed, out_specs=P(BAND, DOM, None, None), check_vma=False
    )
```

```python
from functools import partial

import jax
import jax.numpy as jnp
import numpy as np
from jax import lax
from jax.experimental import pallas as pl
from jax.experimental.pallas import tpu as pltpu
from jax.sharding import Mesh
from jax.sharding import PartitionSpec as P

BAND, DOM = ("y", "x_lo"), ("x_hi", "z_hi", "z_lo", "core")
STAGES = ("y", "x_lo", "core"), ("z_lo",), ("x_hi", "z_hi")

PARTS = 2

HIGHEST = lax.Precision.HIGHEST

spectrum_center = 7.5
spectrum_half = 4.5


def stencil_matrices():
    def band(count):
        away = np.abs(np.arange(count)[:, None] - np.arange(count)[None, :])
        return 16.0 * (away == 1) - 1.0 * (away == 2)

    eye, none = np.eye(32), np.zeros((32, 32))
    own = np.block([[band(32), 16.0 * eye], [16.0 * eye, band(32)]])
    left = np.block([[-eye, 16.0 * eye], [none, -eye]])
    right = np.block([[-eye, none], [16.0 * eye, -eye]])
    across = [np.kron(np.eye(2), part) for part in (left, own, right)]
    return np.concatenate(across, axis=1), band(128) - 90.0 * np.eye(128)


def stencil_kernel(degree, left_ref, cells_ref, right_ref, potential_ref, across_ref, along_ref, *rest):
    out_ref = rest[-1]
    double = 1.0 if degree == 0 else 2.0
    weight = (potential_ref[...] - spectrum_center) * (double / spectrum_half)
    weight = jnp.concatenate([weight, weight], axis=0)
    for step in range(cells_ref.shape[0] // 128):
        rows = slice(128 * step, 128 * step + 128)
        cells = cells_ref[rows, :]
        stack = jnp.concatenate([left_ref[rows, :], cells, right_ref[rows, :]], axis=0)
        laplace = jnp.dot(across_ref[...], stack, preferred_element_type=jnp.float32)
        laplace += jnp.dot(cells, along_ref[...], preferred_element_type=jnp.float32)
        image = weight * cells.astype(jnp.float32) - laplace * (double / (24.0 * spectrum_half))
        if degree > 0:
            image = image - rest[0][rows, :].astype(jnp.float32)
        out_ref[rows, :] = image.astype(jnp.bfloat16)


def filtered_by_one(degree, sides, cells, before, potential, matrices):
    operands = [sides[0], cells, sides[1], potential, *matrices] + ([before] if degree > 0 else [])
    return pl.pallas_call(
        partial(stencil_kernel, degree),
        out_shape=jax.ShapeDtypeStruct(cells.shape, jnp.bfloat16),
        in_specs=[pl.BlockSpec(memory_space=pltpu.VMEM)] * len(operands),
        out_specs=pl.BlockSpec(memory_space=pltpu.VMEM),
        compiler_params=pltpu.CompilerParams(vmem_limit_bytes=32 * 1024 * 1024),
        cost_estimate=pl.CostEstimate(
            flops=1024 * cells.size, bytes_accessed=10 * cells.size, transcendentals=0
        ),
    )(*operands)


def halo(cells):
    count = lax.axis_size(DOM)
    left = lax.ppermute(cells, DOM, [(i, i + 1) for i in range(count - 1)])
    right = lax.ppermute(cells, DOM, [(i + 1, i) for i in range(count - 1)])
    return left, right


def chebyshev(groups, potential):
    matrices = [jnp.asarray(part, jnp.bfloat16) for part in stencil_matrices()]
    latest, previous = list(groups), [None] * len(groups)
    sides = [halo(cells) for cells in latest]
    for degree in range(3):
        for g in range(len(groups)):
            cells = latest[g]
            latest[g] = filtered_by_one(degree, sides[g], cells, previous[g], potential, matrices)
            previous[g] = cells
            if degree < 2:
                sides[g] = halo(latest[g])
    return latest


def dot_nn(a, b):
    return lax.dot_general(a, b, (((1,), (0,)), ((), ())), precision=HIGHEST, preferred_element_type=jnp.float32)


def dot_nt(a, b):
    return lax.dot_general(a, b, (((1,), (1,)), ((), ())), precision=HIGHEST, preferred_element_type=jnp.float32)


def reciprocal(value):
    guess = pl.reciprocal(value, approx=True)
    return guess * (2.0 - value * guess)


def inverse_factor_of_block(rows):
    lane = lax.broadcasted_iota(jnp.int32, (8, 128), 1)
    sub = lax.broadcasted_iota(jnp.int32, (8, 128), 0)
    rows = list(rows)
    out = []
    for p in range(16):
        k0 = 8 * p
        inside = (lane >= k0) & (lane < k0 + 8)
        x = rows[p]
        columns = [jnp.broadcast_to(x[:, k0 + j : k0 + j + 1], (8, 128)) for j in range(8)]
        a = [[jnp.broadcast_to(columns[j][i : i + 1, :], (8, 128)) for j in range(i + 1)] for i in range(8)]
        x = jnp.where(inside, (lane - k0 == sub).astype(jnp.float32), x)
        z = [jnp.broadcast_to(x[i : i + 1, :], (8, 128)) for i in range(8)]
        inv, m = [], [[None] * 8 for _ in range(8)]
        for j in range(8):
            inv.append(reciprocal(a[j][j]))
            for l in range(j + 1, 8):
                m[l][j] = a[l][j] * inv[j]
            for l in range(j + 1, 8):
                for q in range(j + 1, l + 1):
                    a[l][q] = a[l][q] - m[l][j] * a[q][j]
                z[l] = z[l] - m[l][j] * z[j]
        w = z[0] * lax.rsqrt(a[0][0])
        for i in range(1, 8):
            w = jnp.where(sub == i, z[i] * lax.rsqrt(a[i][i]), w)
        out.append(jnp.where(lane < k0 + 8, w, 0.0))
        if p == 15:
            break
        y = [z[j] * inv[j] for j in range(8)]
        for l in range(7, 0, -1):
            for j in range(l):
                y[j] = y[j] - m[l][j] * y[l]
        for i in range(p + 1, 16):
            c = [jnp.broadcast_to(rows[i][:, k0 + j : k0 + j + 1], (8, 128)) for j in range(8)]
            t = [c[j] * y[j] for j in range(8)]
            t = ((t[0] + t[1]) + (t[2] + t[3])) + ((t[4] + t[5]) + (t[6] + t[7]))
            rows[i] = jnp.where(inside, 0.0, rows[i]) - t
    return out


def gram_kernel(field_ref, tiles_ref):
    tile = 0
    for i in range(field_ref.shape[0] // 128):
        rows = slice(128 * i, 128 * i + 128)
        terms = lax.dot_general(
            field_ref[rows, :],
            field_ref[: 128 * i + 128, :],
            (((1,), (1,)), ((), ())),
            preferred_element_type=jnp.float32,
        )
        for j in range(i + 1):
            tiles_ref[128 * tile : 128 * tile + 128, :] = terms[:, 128 * j : 128 * j + 128]
            tile += 1


def gram_tiles(field):
    count = field.shape[0] // 128
    return pl.pallas_call(
        gram_kernel,
        out_shape=jax.ShapeDtypeStruct((64 * count * (count + 1), 128), jnp.float32),
        in_specs=[pl.BlockSpec(memory_space=pltpu.VMEM)],
        out_specs=pl.BlockSpec(memory_space=pltpu.VMEM),
        compiler_params=pltpu.CompilerParams(vmem_limit_bytes=32 * 1024 * 1024),
    )(field)


def rotation_kernel(tiles_ref, field_ref, out_ref, s_ref, a_ref, w_ref, r_ref):
    n, b = field_ref.shape[0], 128
    tile = 0
    for i in range(n // b):
        for j in range(i + 1):
            s_ref[b * i : b * i + b, b * j : b * j + b] = tiles_ref[b * tile : b * tile + b, :]
            tile += 1
    for k in range(n // b):
        lo, hi = k * b, (k + 1) * b
        out = inverse_factor_of_block([s_ref[lo + 8 * i : lo + 8 * i + 8, lo:hi] for i in range(16)])
        for i in range(16):
            w_ref[8 * i : 8 * i + 8, :] = out[i]
        w = w_ref[...]
        r_ref[lo:hi, lo:hi] = w.astype(jnp.bfloat16)
        if hi < n:
            lower = dot_nt(s_ref[hi:, lo:hi], w)
            s_ref[hi:, hi:] -= dot_nt(lower, lower)
        if k > 0:
            v = dot_nn(w, a_ref[lo:hi, :lo])
            r_ref[lo:hi, :lo] = v.astype(jnp.bfloat16)
            if hi < n:
                a_ref[hi:, :lo] -= dot_nn(lower, v)
        if hi < n:
            a_ref[hi:, lo:hi] = -dot_nn(lower, w)
        turned = jnp.dot(r_ref[lo:hi, :hi], field_ref[:hi, :], preferred_element_type=jnp.float32)
        out_ref[lo:hi, :] = turned.astype(jnp.bfloat16)


def rotated_by(tiles, field):
    n = field.shape[0]
    return pl.pallas_call(
        rotation_kernel,
        out_shape=jax.ShapeDtypeStruct(field.shape, jnp.bfloat16),
        in_specs=[pl.BlockSpec(memory_space=pltpu.VMEM)] * 2,
        out_specs=pl.BlockSpec(memory_space=pltpu.VMEM),
        scratch_shapes=[
            pltpu.VMEM((n, n), jnp.float32),
            pltpu.VMEM((n, n), jnp.float32),
            pltpu.VMEM((128, 128), jnp.float32),
            pltpu.VMEM((n, n), jnp.bfloat16),
        ],
        compiler_params=pltpu.CompilerParams(vmem_limit_bytes=32 * 1024 * 1024),
    )(tiles, field)


def exchange(pieces, axis):
    return lax.all_to_all(pieces, axis, 0, 0, tiled=True)


def summed_everywhere(terms, scale):
    part, kept = terms, []
    for axis in STAGES:
        count, rows = lax.axis_size(axis), part.shape[0]
        share = -(-rows // count)
        kept.append((axis, count, share, rows))
        part = jnp.pad(part, ((0, share * count - rows), (0, 0))).reshape(count, share, 128)
        part = jnp.sum(exchange(part, axis), axis=0)
    part = part * scale
    for axis, count, share, rows in reversed(kept):
        part = exchange(jnp.broadcast_to(part[None], (count, share, 128)), axis)
        part = part.reshape(count * share, 128)[:rows]
    return part


def local(orbitals, potential):
    cells_dev = orbitals.shape[1] * orbitals.shape[2] * orbitals.shape[3]
    total_cells = cells_dev * lax.axis_size(DOM)
    slabs = orbitals.reshape(PARTS, -1, orbitals.shape[3])
    filtered = chebyshev([slabs[g] for g in range(PARTS)], potential.reshape(-1, potential.shape[2]))
    flat = jnp.concatenate([part.reshape(-1, cells_dev) for part in filtered], axis=0)
    everyone = lax.all_to_all(flat, BAND, 1, 0, tiled=True)
    tiles = summed_everywhere(gram_tiles(everyone), 1.0 / total_cells)
    turned = rotated_by(tiles, everyone)
    result = lax.all_to_all(turned, BAND, 0, 1, tiled=True)
    return result.reshape(orbitals.shape)


def solution(mesh):
    named = Mesh(mesh.devices.reshape(4, 2, 2, 4, 4, 2), BAND + DOM)
    placed = (P(BAND, DOM, None, None), P(DOM, None, None))
    return jax.shard_map(
        local, mesh=named, in_specs=placed, out_specs=P(BAND, DOM, None, None), check_vma=False
    )
```

```python
from functools import partial

import jax
import jax.numpy as jnp
import numpy as np
from jax import lax
from jax.experimental import pallas as pl
from jax.experimental.pallas import tpu as pltpu
from jax.sharding import Mesh
from jax.sharding import PartitionSpec as P

BAND, DOM = ("y", "x_lo"), ("x_hi", "z", "core")
NEAR, FAR = ("y", "x_lo", "core"), ("x_hi", "z")

BANDS, PARTS = 8, 2

HIGHEST = lax.Precision.HIGHEST

spectrum_center = 7.5
spectrum_half = 4.5


def stencil_matrices():
    def band(count):
        away = np.abs(np.arange(count)[:, None] - np.arange(count)[None, :])
        return 16.0 * (away == 1) - 1.0 * (away == 2)

    eye, none = np.eye(32), np.zeros((32, 32))
    own = np.block([[band(32), 16.0 * eye], [16.0 * eye, band(32)]])
    left = np.block([[-eye, 16.0 * eye], [none, -eye]])
    right = np.block([[-eye, none], [16.0 * eye, -eye]])
    across = [np.kron(np.eye(2), part) for part in (left, own, right)]
    return np.concatenate(across, axis=1), band(128) - 90.0 * np.eye(128)


def stencil_kernel(degree, left_ref, cells_ref, right_ref, potential_ref, across_ref, along_ref, *rest):
    out_ref = rest[-1]
    double = 1.0 if degree == 0 else 2.0
    weight = (potential_ref[...] - spectrum_center) * (double / spectrum_half)
    weight = jnp.concatenate([weight, weight], axis=0)
    for step in range(cells_ref.shape[0] // 128):
        rows = slice(128 * step, 128 * step + 128)
        cells = cells_ref[rows, :]
        stack = jnp.concatenate([left_ref[rows, :], cells, right_ref[rows, :]], axis=0)
        laplace = jnp.dot(across_ref[...], stack, preferred_element_type=jnp.float32)
        laplace += jnp.dot(cells, along_ref[...], preferred_element_type=jnp.float32)
        image = weight * cells.astype(jnp.float32) - laplace * (double / (24.0 * spectrum_half))
        if degree > 0:
            image = image - rest[0][rows, :].astype(jnp.float32)
        out_ref[rows, :] = image.astype(jnp.bfloat16)


def filtered_by_one(degree, sides, cells, before, potential, matrices):
    operands = [sides[0], cells, sides[1], potential, *matrices] + ([before] if degree > 0 else [])
    return pl.pallas_call(
        partial(stencil_kernel, degree),
        out_shape=jax.ShapeDtypeStruct(cells.shape, jnp.bfloat16),
        in_specs=[pl.BlockSpec(memory_space=pltpu.VMEM)] * len(operands),
        out_specs=pl.BlockSpec(memory_space=pltpu.VMEM),
        compiler_params=pltpu.CompilerParams(vmem_limit_bytes=32 * 1024 * 1024),
        cost_estimate=pl.CostEstimate(
            flops=1024 * cells.size, bytes_accessed=10 * cells.size, transcendentals=0
        ),
    )(*operands)


def halo(cells):
    count = lax.axis_size(DOM)
    left = lax.ppermute(cells, DOM, [(i, i + 1) for i in range(count - 1)])
    right = lax.ppermute(cells, DOM, [(i + 1, i) for i in range(count - 1)])
    return left, right


def chebyshev(groups, potential):
    matrices = [jnp.asarray(part, jnp.bfloat16) for part in stencil_matrices()]
    latest, previous = list(groups), [None] * len(groups)
    sides = [halo(cells) for cells in latest]
    for degree in range(3):
        for g in range(len(groups)):
            cells = latest[g]
            latest[g] = filtered_by_one(degree, sides[g], cells, previous[g], potential, matrices)
            previous[g] = cells
            if degree < 2:
                sides[g] = halo(latest[g])
    return latest


def dot_nn(a, b):
    return lax.dot_general(a, b, (((1,), (0,)), ((), ())), precision=HIGHEST, preferred_element_type=jnp.float32)


def dot_nt(a, b):
    return lax.dot_general(a, b, (((1,), (1,)), ((), ())), precision=HIGHEST, preferred_element_type=jnp.float32)


def inverse_factor_of_block(rows):
    lane = lax.broadcasted_iota(jnp.int32, (8, 128), 1)
    sub = lax.broadcasted_iota(jnp.int32, (8, 128), 0)
    rows = list(rows)
    out = []
    for p in range(16):
        k0 = 8 * p
        inside = (lane >= k0) & (lane < k0 + 8)
        x = rows[p]
        columns = [jnp.broadcast_to(x[:, k0 + j : k0 + j + 1], (8, 128)) for j in range(8)]
        a = [[jnp.broadcast_to(columns[j][i : i + 1, :], (8, 128)) for j in range(i + 1)] for i in range(8)]
        x = jnp.where(inside, (lane - k0 == sub).astype(jnp.float32), x)
        z = [jnp.broadcast_to(x[i : i + 1, :], (8, 128)) for i in range(8)]
        inv, m = [], [[None] * 8 for _ in range(8)]
        ahead = []
        if p < 15:
            ahead = [jnp.broadcast_to(rows[p + 1][:, k0 + j : k0 + j + 1], (8, 128)) for j in range(8)]
            following = jnp.where(inside, 0.0, rows[p + 1])
        for j in range(8):
            products = {(l, q): a[l][j] * a[q][j] for l in range(j + 1, 8) for q in range(j + 1, l + 1)}
            inv.append(1.0 / a[j][j])
            for l in range(j + 1, 8):
                m[l][j] = a[l][j] * inv[j]
                for q in range(j + 1, l + 1):
                    a[l][q] = a[l][q] - products[l, q] * inv[j]
                z[l] = z[l] - m[l][j] * z[j]
                if ahead:
                    ahead[l] = ahead[l] - m[l][j] * ahead[j]
            if ahead:
                following = following - (ahead[j] * inv[j]) * z[j]
        w = z[0] * lax.rsqrt(a[0][0])
        for i in range(1, 8):
            w = jnp.where(sub == i, z[i] * lax.rsqrt(a[i][i]), w)
        out.append(jnp.where(lane < k0 + 8, w, 0.0))
        if p == 15:
            break
        y = [z[j] * inv[j] for j in range(8)]
        for l in range(7, 0, -1):
            for j in range(l):
                y[j] = y[j] - m[l][j] * y[l]
        rows[p + 1] = following
        for i in range(p + 2, 16):
            c = [jnp.broadcast_to(rows[i][:, k0 + j : k0 + j + 1], (8, 128)) for j in range(8)]
            t = [c[j] * y[j] for j in range(8)]
            t = ((t[0] + t[1]) + (t[2] + t[3])) + ((t[4] + t[5]) + (t[6] + t[7]))
            rows[i] = jnp.where(inside, 0.0, rows[i]) - t
    return out


def gram_kernel(*refs):
    part_refs, field_ref, tiles_ref = refs[:-2], refs[-2], refs[-1]
    rows = part_refs[0].shape[0] // BANDS
    for band in range(BANDS):
        for part, part_ref in enumerate(part_refs):
            at = (band * len(part_refs) + part) * rows
            field_ref[at : at + rows, :] = part_ref[band * rows : band * rows + rows, :]
    tile = 0
    for i in range(field_ref.shape[0] // 128):
        terms = lax.dot_general(
            field_ref[128 * i : 128 * i + 128, :],
            field_ref[: 128 * i + 128, :],
            (((1,), (1,)), ((), ())),
            preferred_element_type=jnp.float32,
        )
        for j in range(i + 1):
            tiles_ref[128 * tile : 128 * tile + 128, :] = terms[:, 128 * j : 128 * j + 128]
            tile += 1


def field_and_tiles(parts):
    rows = sum(part.shape[0] for part in parts)
    count = rows // 128
    return pl.pallas_call(
        gram_kernel,
        out_shape=[
            jax.ShapeDtypeStruct((rows, parts[0].shape[1]), jnp.bfloat16),
            jax.ShapeDtypeStruct((64 * count * (count + 1), 128), jnp.float32),
        ],
        in_specs=[pl.BlockSpec(memory_space=pltpu.VMEM)] * len(parts),
        out_specs=[pl.BlockSpec(memory_space=pltpu.VMEM)] * 2,
        compiler_params=pltpu.CompilerParams(vmem_limit_bytes=32 * 1024 * 1024),
    )(*parts)


def rotation_kernel(tiles_ref, field_ref, out_ref, s_ref, a_ref, w_ref, r_ref):
    n, b = field_ref.shape[0], 128
    tile = 0
    for i in range(n // b):
        for j in range(i + 1):
            s_ref[b * i : b * i + b, b * j : b * j + b] = tiles_ref[b * tile : b * tile + b, :]
            tile += 1
    for k in range(n // b):
        lo, hi = k * b, (k + 1) * b
        out = inverse_factor_of_block([s_ref[lo + 8 * i : lo + 8 * i + 8, lo:hi] for i in range(16)])
        for i in range(16):
            w_ref[8 * i : 8 * i + 8, :] = out[i]
        w = w_ref[...]
        r_ref[lo:hi, lo:hi] = w.astype(jnp.bfloat16)
        if hi < n:
            lower = dot_nt(s_ref[hi:, lo:hi], w)
            s_ref[hi:, hi:] -= dot_nt(lower, lower)
        if k > 0:
            v = dot_nn(w, a_ref[lo:hi, :lo])
            r_ref[lo:hi, :lo] = v.astype(jnp.bfloat16)
            if hi < n:
                a_ref[hi:, :lo] -= dot_nn(lower, v)
        if hi < n:
            a_ref[hi:, lo:hi] = -dot_nn(lower, w)
        turned = jnp.dot(r_ref[lo:hi, :hi], field_ref[:hi, :], preferred_element_type=jnp.float32)
        out_ref[lo:hi, :] = turned.astype(jnp.bfloat16)


def rotated_by(tiles, field):
    n = field.shape[0]
    return pl.pallas_call(
        rotation_kernel,
        out_shape=jax.ShapeDtypeStruct(field.shape, jnp.bfloat16),
        in_specs=[pl.BlockSpec(memory_space=pltpu.VMEM)] * 2,
        out_specs=pl.BlockSpec(memory_space=pltpu.VMEM),
        scratch_shapes=[
            pltpu.VMEM((n, n), jnp.float32),
            pltpu.VMEM((n, n), jnp.float32),
            pltpu.VMEM((128, 128), jnp.float32),
            pltpu.VMEM((n, n), jnp.bfloat16),
        ],
        compiler_params=pltpu.CompilerParams(vmem_limit_bytes=32 * 1024 * 1024),
    )(tiles, field)


def exchange(pieces, axis):
    return lax.all_to_all(pieces, axis, 0, 0, tiled=True)


def summed_everywhere(terms, scale):
    first, second = lax.axis_size(NEAR), lax.axis_size(FAR)
    rows = terms.shape[0] // first
    share = -(-rows // second)
    part = jnp.sum(exchange(terms.reshape(first, rows, 128), NEAR), axis=0)
    part = jnp.pad(part, ((0, share * second - rows), (0, 0))).reshape(second, share, 128)
    own = jnp.sum(exchange(part, FAR), axis=0, keepdims=True) * scale
    part = exchange(jnp.broadcast_to(own, (second, share, 128)), FAR)
    part = part.reshape(share * second, 128)[:rows]
    return exchange(jnp.broadcast_to(part[None], (first, rows, 128)), NEAR).reshape(terms.shape)


def local(orbitals, potential):
    cells_dev = orbitals.shape[1] * orbitals.shape[2] * orbitals.shape[3]
    total_cells = cells_dev * lax.axis_size(DOM)
    slabs = orbitals.reshape(PARTS, -1, orbitals.shape[3])
    filtered = chebyshev([slabs[g] for g in range(PARTS)], potential.reshape(-1, potential.shape[2]))
    shares = [
        lax.all_to_all(part.reshape(-1, cells_dev), BAND, 1, 0, tiled=True) for part in filtered
    ]
    everyone, terms = field_and_tiles(shares)
    tiles = summed_everywhere(terms, 1.0 / total_cells)
    turned = rotated_by(tiles, everyone)
    result = lax.all_to_all(turned, BAND, 0, 1, tiled=True)
    return result.reshape(orbitals.shape)


def solution(mesh):
    named = Mesh(mesh.devices.reshape(4, 2, 2, 16, 2), ("y", "x_lo", "x_hi", "z", "core"))
    placed = (P(BAND, DOM, None, None), P(DOM, None, None))
    return jax.shard_map(
        local, mesh=named, in_specs=placed, out_specs=P(BAND, DOM, None, None), check_vma=False
    )
```

```python
from functools import partial

import jax
import jax.numpy as jnp
import numpy as np
from jax import lax
from jax.experimental import pallas as pl
from jax.experimental.pallas import tpu as pltpu
from jax.sharding import Mesh
from jax.sharding import PartitionSpec as P

BAND, DOM = ("y", "x_lo"), ("x_hi", "z", "core")
NEAR = ("y", "x_lo", "core")

BANDS, PARTS = 8, 2

HIGHEST = lax.Precision.HIGHEST

spectrum_center = 7.5
spectrum_half = 4.5


def stencil_matrices():
    def band(count):
        away = np.abs(np.arange(count)[:, None] - np.arange(count)[None, :])
        return 16.0 * (away == 1) - 1.0 * (away == 2)

    eye, none = np.eye(32), np.zeros((32, 32))
    own = np.block([[band(32), 16.0 * eye], [16.0 * eye, band(32)]])
    left = np.block([[-eye, 16.0 * eye], [none, -eye]])
    right = np.block([[-eye, none], [16.0 * eye, -eye]])
    across = [np.kron(np.eye(2), part) for part in (left, own, right)]
    return np.concatenate(across, axis=1), band(128) - 90.0 * np.eye(128)


def stencil_kernel(degree, left_ref, cells_ref, right_ref, potential_ref, across_ref, along_ref, *rest):
    out_ref = rest[-1]
    double = 1.0 if degree == 0 else 2.0
    weight = (potential_ref[...] - spectrum_center) * (double / spectrum_half)
    weight = jnp.concatenate([weight, weight], axis=0)
    for step in range(cells_ref.shape[0] // 128):
        rows = slice(128 * step, 128 * step + 128)
        cells = cells_ref[rows, :]
        stack = jnp.concatenate([left_ref[rows, :], cells, right_ref[rows, :]], axis=0)
        laplace = jnp.dot(across_ref[...], stack, preferred_element_type=jnp.float32)
        laplace += jnp.dot(cells, along_ref[...], preferred_element_type=jnp.float32)
        image = weight * cells.astype(jnp.float32) - laplace * (double / (24.0 * spectrum_half))
        if degree > 0:
            image = image - rest[0][rows, :].astype(jnp.float32)
        out_ref[rows, :] = image.astype(jnp.bfloat16)


def filtered_by_one(degree, sides, cells, before, potential, matrices):
    operands = [sides[0], cells, sides[1], potential, *matrices] + ([before] if degree > 0 else [])
    return pl.pallas_call(
        partial(stencil_kernel, degree),
        out_shape=jax.ShapeDtypeStruct(cells.shape, jnp.bfloat16),
        in_specs=[pl.BlockSpec(memory_space=pltpu.VMEM)] * len(operands),
        out_specs=pl.BlockSpec(memory_space=pltpu.VMEM),
        compiler_params=pltpu.CompilerParams(vmem_limit_bytes=32 * 1024 * 1024),
        cost_estimate=pl.CostEstimate(
            flops=1024 * cells.size, bytes_accessed=10 * cells.size, transcendentals=0
        ),
    )(*operands)


def halo(cells):
    count = lax.axis_size(DOM)
    left = lax.ppermute(cells, DOM, [(i, i + 1) for i in range(count - 1)])
    right = lax.ppermute(cells, DOM, [(i + 1, i) for i in range(count - 1)])
    return left, right


def chebyshev(groups, potential):
    matrices = [jnp.asarray(part, jnp.bfloat16) for part in stencil_matrices()]
    latest, previous = list(groups), [None] * len(groups)
    sides = [halo(cells) for cells in latest]
    for degree in range(3):
        for g in range(len(groups)):
            cells = latest[g]
            latest[g] = filtered_by_one(degree, sides[g], cells, previous[g], potential, matrices)
            previous[g] = cells
            if degree < 2:
                sides[g] = halo(latest[g])
    return latest


def dot_nn(a, b):
    return lax.dot_general(a, b, (((1,), (0,)), ((), ())), precision=HIGHEST, preferred_element_type=jnp.float32)


def dot_nt(a, b):
    return lax.dot_general(a, b, (((1,), (1,)), ((), ())), precision=HIGHEST, preferred_element_type=jnp.float32)


def inverse_factor_of_block(rows):
    lane = lax.broadcasted_iota(jnp.int32, (8, 128), 1)
    sub = lax.broadcasted_iota(jnp.int32, (8, 128), 0)
    rows = list(rows)
    out = []
    for p in range(16):
        k0 = 8 * p
        inside = (lane >= k0) & (lane < k0 + 8)
        x = rows[p]
        columns = [jnp.broadcast_to(x[:, k0 + j : k0 + j + 1], (8, 128)) for j in range(8)]
        a = [[jnp.broadcast_to(columns[j][i : i + 1, :], (8, 128)) for j in range(i + 1)] for i in range(8)]
        x = jnp.where(inside, (lane - k0 == sub).astype(jnp.float32), x)
        z = [jnp.broadcast_to(x[i : i + 1, :], (8, 128)) for i in range(8)]
        inv, m = [], [[None] * 8 for _ in range(8)]
        ahead = []
        if p < 15:
            ahead = [jnp.broadcast_to(rows[p + 1][:, k0 + j : k0 + j + 1], (8, 128)) for j in range(8)]
            following = jnp.where(inside, 0.0, rows[p + 1])
        for j in range(8):
            products = {(l, q): a[l][j] * a[q][j] for l in range(j + 1, 8) for q in range(j + 1, l + 1)}
            inv.append(1.0 / a[j][j])
            for l in range(j + 1, 8):
                m[l][j] = a[l][j] * inv[j]
                for q in range(j + 1, l + 1):
                    a[l][q] = a[l][q] - products[l, q] * inv[j]
                z[l] = z[l] - m[l][j] * z[j]
                if ahead:
                    ahead[l] = ahead[l] - m[l][j] * ahead[j]
            if ahead:
                following = following - (ahead[j] * inv[j]) * z[j]
        w = z[0] * lax.rsqrt(a[0][0])
        for i in range(1, 8):
            w = jnp.where(sub == i, z[i] * lax.rsqrt(a[i][i]), w)
        out.append(jnp.where(lane < k0 + 8, w, 0.0))
        if p == 15:
            break
        y = [z[j] * inv[j] for j in range(8)]
        for l in range(7, 0, -1):
            for j in range(l):
                y[j] = y[j] - m[l][j] * y[l]
        rows[p + 1] = following
        for i in range(p + 2, 16):
            c = [jnp.broadcast_to(rows[i][:, k0 + j : k0 + j + 1], (8, 128)) for j in range(8)]
            t = [c[j] * y[j] for j in range(8)]
            t = ((t[0] + t[1]) + (t[2] + t[3])) + ((t[4] + t[5]) + (t[6] + t[7]))
            rows[i] = jnp.where(inside, 0.0, rows[i]) - t
    return out


def gram_kernel(*refs):
    part_refs, field_ref, tiles_ref = refs[:-2], refs[-2], refs[-1]
    rows = part_refs[0].shape[0] // BANDS
    for band in range(BANDS):
        for part, part_ref in enumerate(part_refs):
            at = (band * len(part_refs) + part) * rows
            field_ref[at : at + rows, :] = part_ref[band * rows : band * rows + rows, :]
    tile = 0
    for i in range(field_ref.shape[0] // 128):
        terms = lax.dot_general(
            field_ref[128 * i : 128 * i + 128, :],
            field_ref[: 128 * i + 128, :],
            (((1,), (1,)), ((), ())),
            preferred_element_type=jnp.float32,
        )
        for j in range(i + 1):
            tiles_ref[128 * tile : 128 * tile + 128, :] = terms[:, 128 * j : 128 * j + 128]
            tile += 1


def field_and_tiles(parts):
    rows = sum(part.shape[0] for part in parts)
    count = rows // 128
    return pl.pallas_call(
        gram_kernel,
        out_shape=[
            jax.ShapeDtypeStruct((rows, parts[0].shape[1]), jnp.bfloat16),
            jax.ShapeDtypeStruct((64 * count * (count + 1), 128), jnp.float32),
        ],
        in_specs=[pl.BlockSpec(memory_space=pltpu.VMEM)] * len(parts),
        out_specs=[pl.BlockSpec(memory_space=pltpu.VMEM)] * 2,
        compiler_params=pltpu.CompilerParams(vmem_limit_bytes=32 * 1024 * 1024),
    )(*parts)


def rotation_kernel(tiles_ref, field_ref, out_ref, s_ref, a_ref, w_ref, r_ref):
    n, b = field_ref.shape[0], 128
    tile = 0
    for i in range(n // b):
        for j in range(i + 1):
            s_ref[b * i : b * i + b, b * j : b * j + b] = tiles_ref[b * tile : b * tile + b, :]
            tile += 1
    for k in range(n // b):
        lo, hi = k * b, (k + 1) * b
        out = inverse_factor_of_block([s_ref[lo + 8 * i : lo + 8 * i + 8, lo:hi] for i in range(16)])
        for i in range(16):
            w_ref[8 * i : 8 * i + 8, :] = out[i]
        w = w_ref[...]
        r_ref[lo:hi, lo:hi] = w.astype(jnp.bfloat16)
        if hi < n:
            lower = dot_nt(s_ref[hi:, lo:hi], w)
            s_ref[hi:, hi:] -= dot_nt(lower, lower)
        if k > 0:
            v = dot_nn(w, a_ref[lo:hi, :lo])
            r_ref[lo:hi, :lo] = v.astype(jnp.bfloat16)
            if hi < n:
                a_ref[hi:, :lo] -= dot_nn(lower, v)
        if hi < n:
            a_ref[hi:, lo:hi] = -dot_nn(lower, w)
        turned = jnp.dot(r_ref[lo:hi, :hi], field_ref[:hi, :], preferred_element_type=jnp.float32)
        out_ref[lo:hi, :] = turned.astype(jnp.bfloat16)


def rotated_by(tiles, field):
    n = field.shape[0]
    return pl.pallas_call(
        rotation_kernel,
        out_shape=jax.ShapeDtypeStruct(field.shape, jnp.bfloat16),
        in_specs=[pl.BlockSpec(memory_space=pltpu.VMEM)] * 2,
        out_specs=pl.BlockSpec(memory_space=pltpu.VMEM),
        scratch_shapes=[
            pltpu.VMEM((n, n), jnp.float32),
            pltpu.VMEM((n, n), jnp.float32),
            pltpu.VMEM((128, 128), jnp.float32),
            pltpu.VMEM((n, n), jnp.bfloat16),
        ],
        compiler_params=pltpu.CompilerParams(vmem_limit_bytes=32 * 1024 * 1024),
    )(tiles, field)


def exchange(pieces, axis):
    return lax.all_to_all(pieces, axis, 0, 0, tiled=True)


def summed_everywhere(terms, scale):
    near, far = lax.axis_size(NEAR), lax.axis_size("z")
    rows = terms.shape[0] // near
    part = jnp.sum(exchange(terms.reshape(near, rows, 128), NEAR), axis=0)
    part = jnp.sum(exchange(part.reshape(far, rows // far, 128), "z"), axis=0)
    part = (part + lax.ppermute(part, "x_hi", [(0, 1), (1, 0)])) * scale
    part = exchange(jnp.broadcast_to(part[None], (far,) + part.shape), "z").reshape(rows, 128)
    return exchange(jnp.broadcast_to(part[None], (near, rows, 128)), NEAR).reshape(terms.shape)


def local(orbitals, potential):
    cells_dev = orbitals.shape[1] * orbitals.shape[2] * orbitals.shape[3]
    total_cells = cells_dev * lax.axis_size(DOM)
    slabs = orbitals.reshape(PARTS, -1, orbitals.shape[3])
    filtered = chebyshev([slabs[g] for g in range(PARTS)], potential.reshape(-1, potential.shape[2]))
    shares = [
        lax.all_to_all(part.reshape(-1, cells_dev), BAND, 1, 0, tiled=True) for part in filtered
    ]
    everyone, terms = field_and_tiles(shares)
    tiles = summed_everywhere(terms, 1.0 / total_cells)
    turned = rotated_by(tiles, everyone)
    result = lax.all_to_all(turned, BAND, 0, 1, tiled=True)
    return result.reshape(orbitals.shape)


def solution(mesh):
    named = Mesh(mesh.devices.reshape(4, 2, 2, 16, 2), ("y", "x_lo", "x_hi", "z", "core"))
    placed = (P(BAND, DOM, None, None), P(DOM, None, None))
    return jax.shard_map(
        local, mesh=named, in_specs=placed, out_specs=P(BAND, DOM, None, None), check_vma=False
    )
```

```python
from functools import partial

import jax
import jax.numpy as jnp
import numpy as np
from jax import lax
from jax.experimental import pallas as pl
from jax.experimental.pallas import tpu as pltpu
from jax.sharding import Mesh
from jax.sharding import PartitionSpec as P

BAND, DOM = ("y", "x_lo"), ("x_hi", "z_hi", "z_lo", "core")

BANDS, PARTS = 8, 2

HIGHEST = lax.Precision.HIGHEST

spectrum_center = 7.5
spectrum_half = 4.5


def stencil_matrices():
    def band(count):
        away = np.abs(np.arange(count)[:, None] - np.arange(count)[None, :])
        return 16.0 * (away == 1) - 1.0 * (away == 2)

    eye, none = np.eye(32), np.zeros((32, 32))
    own = np.block([[band(32), 16.0 * eye], [16.0 * eye, band(32)]])
    left = np.block([[-eye, 16.0 * eye], [none, -eye]])
    right = np.block([[-eye, none], [16.0 * eye, -eye]])
    across = [np.kron(np.eye(2), part) for part in (left, own, right)]
    return np.concatenate(across, axis=1), band(128) - 90.0 * np.eye(128)


def stencil_kernel(degree, left_ref, cells_ref, right_ref, potential_ref, across_ref, along_ref, *rest):
    out_ref = rest[-1]
    double = 1.0 if degree == 0 else 2.0
    weight = (potential_ref[...] - spectrum_center) * (double / spectrum_half)
    weight = jnp.concatenate([weight, weight], axis=0)
    for step in range(cells_ref.shape[0] // 128):
        rows = slice(128 * step, 128 * step + 128)
        cells = cells_ref[rows, :]
        stack = jnp.concatenate([left_ref[rows, :], cells, right_ref[rows, :]], axis=0)
        laplace = jnp.dot(across_ref[...], stack, preferred_element_type=jnp.float32)
        laplace += jnp.dot(cells, along_ref[...], preferred_element_type=jnp.float32)
        image = weight * cells.astype(jnp.float32) - laplace * (double / (24.0 * spectrum_half))
        if degree > 0:
            image = image - rest[0][rows, :].astype(jnp.float32)
        out_ref[rows, :] = image.astype(jnp.bfloat16)


def filtered_by_one(degree, sides, cells, before, potential, matrices):
    operands = [sides[0], cells, sides[1], potential, *matrices] + ([before] if degree > 0 else [])
    return pl.pallas_call(
        partial(stencil_kernel, degree),
        out_shape=jax.ShapeDtypeStruct(cells.shape, jnp.bfloat16),
        in_specs=[pl.BlockSpec(memory_space=pltpu.VMEM)] * len(operands),
        out_specs=pl.BlockSpec(memory_space=pltpu.VMEM),
        compiler_params=pltpu.CompilerParams(vmem_limit_bytes=32 * 1024 * 1024),
        cost_estimate=pl.CostEstimate(
            flops=1024 * cells.size, bytes_accessed=10 * cells.size, transcendentals=0
        ),
    )(*operands)


def halo(cells):
    count = lax.axis_size(DOM)
    left = lax.ppermute(cells, DOM, [(i, i + 1) for i in range(count - 1)])
    right = lax.ppermute(cells, DOM, [(i + 1, i) for i in range(count - 1)])
    return left, right


def chebyshev(groups, potential):
    matrices = [jnp.asarray(part, jnp.bfloat16) for part in stencil_matrices()]
    latest, previous = list(groups), [None] * len(groups)
    sides = [halo(cells) for cells in latest]
    for degree in range(3):
        for g in range(len(groups)):
            cells = latest[g]
            latest[g] = filtered_by_one(degree, sides[g], cells, previous[g], potential, matrices)
            previous[g] = cells
            if degree < 2:
                sides[g] = halo(latest[g])
    return latest


def dot_nn(a, b):
    return lax.dot_general(a, b, (((1,), (0,)), ((), ())), precision=HIGHEST, preferred_element_type=jnp.float32)


def dot_nt(a, b):
    return lax.dot_general(a, b, (((1,), (1,)), ((), ())), precision=HIGHEST, preferred_element_type=jnp.float32)


def inverse_factor_of_block(rows):
    lane = lax.broadcasted_iota(jnp.int32, (8, 128), 1)
    sub = lax.broadcasted_iota(jnp.int32, (8, 128), 0)
    rows = list(rows)
    out = []
    for p in range(16):
        k0 = 8 * p
        inside = (lane >= k0) & (lane < k0 + 8)
        x = rows[p]
        columns = [jnp.broadcast_to(x[:, k0 + j : k0 + j + 1], (8, 128)) for j in range(8)]
        a = [[jnp.broadcast_to(columns[j][i : i + 1, :], (8, 128)) for j in range(i + 1)] for i in range(8)]
        x = jnp.where(inside, (lane - k0 == sub).astype(jnp.float32), x)
        z = [jnp.broadcast_to(x[i : i + 1, :], (8, 128)) for i in range(8)]
        inv, m = [], [[None] * 8 for _ in range(8)]
        ahead = []
        if p < 15:
            ahead = [jnp.broadcast_to(rows[p + 1][:, k0 + j : k0 + j + 1], (8, 128)) for j in range(8)]
            following = jnp.where(inside, 0.0, rows[p + 1])
        for j in range(8):
            products = {(l, q): a[l][j] * a[q][j] for l in range(j + 1, 8) for q in range(j + 1, l + 1)}
            inv.append(1.0 / a[j][j])
            for l in range(j + 1, 8):
                m[l][j] = a[l][j] * inv[j]
                for q in range(j + 1, l + 1):
                    a[l][q] = a[l][q] - products[l, q] * inv[j]
                z[l] = z[l] - m[l][j] * z[j]
                if ahead:
                    ahead[l] = ahead[l] - m[l][j] * ahead[j]
            if ahead:
                following = following - (ahead[j] * inv[j]) * z[j]
        w = z[0] * lax.rsqrt(a[0][0])
        for i in range(1, 8):
            w = jnp.where(sub == i, z[i] * lax.rsqrt(a[i][i]), w)
        out.append(jnp.where(lane < k0 + 8, w, 0.0))
        if p == 15:
            break
        y = [z[j] * inv[j] for j in range(8)]
        for l in range(7, 0, -1):
            for j in range(l):
                y[j] = y[j] - m[l][j] * y[l]
        rows[p + 1] = following
        for i in range(p + 2, 16):
            c = [jnp.broadcast_to(rows[i][:, k0 + j : k0 + j + 1], (8, 128)) for j in range(8)]
            t = [c[j] * y[j] for j in range(8)]
            t = ((t[0] + t[1]) + (t[2] + t[3])) + ((t[4] + t[5]) + (t[6] + t[7]))
            rows[i] = jnp.where(inside, 0.0, rows[i]) - t
    return out


def gram_kernel(*refs):
    part_refs, field_ref, tiles_ref = refs[:-2], refs[-2], refs[-1]
    rows = part_refs[0].shape[0] // BANDS
    for band in range(BANDS):
        for part, part_ref in enumerate(part_refs):
            at = (band * len(part_refs) + part) * rows
            field_ref[at : at + rows, :] = part_ref[band * rows : band * rows + rows, :]
    tile = 0
    for i in range(field_ref.shape[0] // 128):
        terms = lax.dot_general(
            field_ref[128 * i : 128 * i + 128, :],
            field_ref[: 128 * i + 128, :],
            (((1,), (1,)), ((), ())),
            preferred_element_type=jnp.float32,
        )
        for j in range(i + 1):
            tiles_ref[128 * tile : 128 * tile + 128, :] = terms[:, 128 * j : 128 * j + 128]
            tile += 1


def field_and_tiles(parts):
    rows = sum(part.shape[0] for part in parts)
    count = rows // 128
    return pl.pallas_call(
        gram_kernel,
        out_shape=[
            jax.ShapeDtypeStruct((rows, parts[0].shape[1]), jnp.bfloat16),
            jax.ShapeDtypeStruct((64 * count * (count + 1), 128), jnp.float32),
        ],
        in_specs=[pl.BlockSpec(memory_space=pltpu.VMEM)] * len(parts),
        out_specs=[pl.BlockSpec(memory_space=pltpu.VMEM)] * 2,
        compiler_params=pltpu.CompilerParams(vmem_limit_bytes=32 * 1024 * 1024),
    )(*parts)


def rotation_kernel(tiles_ref, field_ref, out_ref, s_ref, a_ref, w_ref, r_ref):
    n, b = field_ref.shape[0], 128
    tile = 0
    for i in range(n // b):
        for j in range(i + 1):
            s_ref[b * i : b * i + b, b * j : b * j + b] = tiles_ref[b * tile : b * tile + b, :]
            tile += 1
    for k in range(n // b):
        lo, hi = k * b, (k + 1) * b
        out = inverse_factor_of_block([s_ref[lo + 8 * i : lo + 8 * i + 8, lo:hi] for i in range(16)])
        for i in range(16):
            w_ref[8 * i : 8 * i + 8, :] = out[i]
        w = w_ref[...]
        r_ref[lo:hi, lo:hi] = w.astype(jnp.bfloat16)
        if hi < n:
            lower = dot_nt(s_ref[hi:, lo:hi], w)
            s_ref[hi:, hi:] -= dot_nt(lower, lower)
        if k > 0:
            v = dot_nn(w, a_ref[lo:hi, :lo])
            r_ref[lo:hi, :lo] = v.astype(jnp.bfloat16)
            if hi < n:
                a_ref[hi:, :lo] -= dot_nn(lower, v)
        if hi < n:
            a_ref[hi:, lo:hi] = -dot_nn(lower, w)
        turned = jnp.dot(r_ref[lo:hi, :hi], field_ref[:hi, :], preferred_element_type=jnp.float32)
        out_ref[lo:hi, :] = turned.astype(jnp.bfloat16)


def rotated_by(tiles, field):
    n = field.shape[0]
    return pl.pallas_call(
        rotation_kernel,
        out_shape=jax.ShapeDtypeStruct(field.shape, jnp.bfloat16),
        in_specs=[pl.BlockSpec(memory_space=pltpu.VMEM)] * 2,
        out_specs=pl.BlockSpec(memory_space=pltpu.VMEM),
        scratch_shapes=[
            pltpu.VMEM((n, n), jnp.float32),
            pltpu.VMEM((n, n), jnp.float32),
            pltpu.VMEM((128, 128), jnp.float32),
            pltpu.VMEM((n, n), jnp.bfloat16),
        ],
        compiler_params=pltpu.CompilerParams(vmem_limit_bytes=32 * 1024 * 1024),
    )(tiles, field)


def exchange(pieces, axis):
    return lax.all_to_all(pieces, axis, 0, 0, tiled=True)


def scattered_sum(part, axis):
    count = lax.axis_size(axis)
    return jnp.sum(exchange(part.reshape(count, part.shape[0] // count, 128), axis), axis=0)


def spread(part, axis):
    count, rows = lax.axis_size(axis), part.shape[0]
    return exchange(jnp.broadcast_to(part[None], (count, rows, 128)), axis).reshape(count * rows, 128)


def shifted(part, axis, by):
    count = lax.axis_size(axis)
    return lax.ppermute(part, axis, [(i, (i + by) % count) for i in range(count)])


def summed_everywhere(terms, scale):
    part = scattered_sum(scattered_sum(scattered_sum(terms, "core"), BAND), "z_lo")
    part = (part + shifted(part, "z_hi", 2)) + (shifted(part, "z_hi", 1) + shifted(part, "z_hi", 3))
    part = (part + shifted(part, "x_hi", 1)) * scale
    return lax.all_gather(spread(spread(part, "z_lo"), BAND), "core", axis=0, tiled=True)


def local(orbitals, potential):
    cells_dev = orbitals.shape[1] * orbitals.shape[2] * orbitals.shape[3]
    total_cells = cells_dev * lax.axis_size(DOM)
    slabs = orbitals.reshape(PARTS, -1, orbitals.shape[3])
    filtered = chebyshev([slabs[g] for g in range(PARTS)], potential.reshape(-1, potential.shape[2]))
    shares = [
        lax.all_to_all(part.reshape(-1, cells_dev), BAND, 1, 0, tiled=True) for part in filtered
    ]
    everyone, terms = field_and_tiles(shares)
    tiles = summed_everywhere(terms, 1.0 / total_cells)
    turned = rotated_by(tiles, everyone)
    result = lax.all_to_all(turned, BAND, 0, 1, tiled=True)
    return result.reshape(orbitals.shape)


def solution(mesh):
    named = Mesh(mesh.devices.reshape(4, 2, 2, 4, 4, 2), BAND + DOM)
    placed = (P(BAND, DOM, None, None), P(DOM, None, None))
    return jax.shard_map(
        local, mesh=named, in_specs=placed, out_specs=P(BAND, DOM, None, None), check_vma=False
    )
```

```python
from functools import partial

import jax
import jax.numpy as jnp
import numpy as np
from jax import lax
from jax.experimental import pallas as pl
from jax.experimental.pallas import tpu as pltpu
from jax.sharding import Mesh
from jax.sharding import PartitionSpec as P

BAND, DOM = ("y", "x_lo"), ("x_hi", "z", "core")
NEAR = ("core", "y", "x_lo")

BANDS, PARTS = 8, 2

HIGHEST = lax.Precision.HIGHEST

spectrum_center = 7.5
spectrum_half = 4.5


def stencil_matrices():
    def band(count):
        away = np.abs(np.arange(count)[:, None] - np.arange(count)[None, :])
        return 16.0 * (away == 1) - 1.0 * (away == 2)

    eye, none = np.eye(32), np.zeros((32, 32))
    own = np.block([[band(32), 16.0 * eye], [16.0 * eye, band(32)]])
    left = np.block([[-eye, 16.0 * eye], [none, -eye]])
    right = np.block([[-eye, none], [16.0 * eye, -eye]])
    across = [np.kron(np.eye(2), part) for part in (left, own, right)]
    return np.concatenate(across, axis=1), band(128) - 90.0 * np.eye(128)


def stencil_kernel(degree, left_ref, cells_ref, right_ref, potential_ref, across_ref, along_ref, *rest):
    out_ref = rest[-1]
    double = 1.0 if degree == 0 else 2.0
    weight = (potential_ref[...] - spectrum_center) * (double / spectrum_half)
    weight = jnp.concatenate([weight, weight], axis=0)
    for step in range(cells_ref.shape[0] // 128):
        rows = slice(128 * step, 128 * step + 128)
        cells = cells_ref[rows, :]
        stack = jnp.concatenate([left_ref[rows, :], cells, right_ref[rows, :]], axis=0)
        laplace = jnp.dot(across_ref[...], stack, preferred_element_type=jnp.float32)
        laplace += jnp.dot(cells, along_ref[...], preferred_element_type=jnp.float32)
        image = weight * cells.astype(jnp.float32) - laplace * (double / (24.0 * spectrum_half))
        if degree > 0:
            image = image - rest[0][rows, :].astype(jnp.float32)
        out_ref[rows, :] = image.astype(jnp.bfloat16)


def filtered_by_one(degree, sides, cells, before, potential, matrices):
    operands = [sides[0], cells, sides[1], potential, *matrices] + ([before] if degree > 0 else [])
    return pl.pallas_call(
        partial(stencil_kernel, degree),
        out_shape=jax.ShapeDtypeStruct(cells.shape, jnp.bfloat16),
        in_specs=[pl.BlockSpec(memory_space=pltpu.VMEM)] * len(operands),
        out_specs=pl.BlockSpec(memory_space=pltpu.VMEM),
        compiler_params=pltpu.CompilerParams(vmem_limit_bytes=32 * 1024 * 1024),
        cost_estimate=pl.CostEstimate(
            flops=1024 * cells.size, bytes_accessed=10 * cells.size, transcendentals=0
        ),
    )(*operands)


def halo(cells):
    count = lax.axis_size(DOM)
    left = lax.ppermute(cells, DOM, [(i, i + 1) for i in range(count - 1)])
    right = lax.ppermute(cells, DOM, [(i + 1, i) for i in range(count - 1)])
    return left, right


def chebyshev(groups, potential):
    matrices = [jnp.asarray(part, jnp.bfloat16) for part in stencil_matrices()]
    latest, previous = list(groups), [None] * len(groups)
    sides = [halo(cells) for cells in latest]
    for degree in range(3):
        for g in range(len(groups)):
            cells = latest[g]
            latest[g] = filtered_by_one(degree, sides[g], cells, previous[g], potential, matrices)
            previous[g] = cells
            if degree < 2:
                sides[g] = halo(latest[g])
    return latest


def dot_nn(a, b):
    return lax.dot_general(a, b, (((1,), (0,)), ((), ())), precision=HIGHEST, preferred_element_type=jnp.float32)


def dot_nt(a, b):
    return lax.dot_general(a, b, (((1,), (1,)), ((), ())), precision=HIGHEST, preferred_element_type=jnp.float32)


def inverse_factor_of_block(rows):
    lane = lax.broadcasted_iota(jnp.int32, (8, 128), 1)
    sub = lax.broadcasted_iota(jnp.int32, (8, 128), 0)
    rows = list(rows)
    out = []
    for p in range(16):
        k0 = 8 * p
        inside = (lane >= k0) & (lane < k0 + 8)
        x = rows[p]
        columns = [jnp.broadcast_to(x[:, k0 + j : k0 + j + 1], (8, 128)) for j in range(8)]
        a = [[jnp.broadcast_to(columns[j][i : i + 1, :], (8, 128)) for j in range(i + 1)] for i in range(8)]
        x = jnp.where(inside, (lane - k0 == sub).astype(jnp.float32), x)
        z = [jnp.broadcast_to(x[i : i + 1, :], (8, 128)) for i in range(8)]
        inv, m = [], [[None] * 8 for _ in range(8)]
        ahead = []
        if p < 15:
            ahead = [jnp.broadcast_to(rows[p + 1][:, k0 + j : k0 + j + 1], (8, 128)) for j in range(8)]
            following = jnp.where(inside, 0.0, rows[p + 1])
        for j in range(8):
            products = {(l, q): a[l][j] * a[q][j] for l in range(j + 1, 8) for q in range(j + 1, l + 1)}
            inv.append(1.0 / a[j][j])
            for l in range(j + 1, 8):
                m[l][j] = a[l][j] * inv[j]
                for q in range(j + 1, l + 1):
                    a[l][q] = a[l][q] - products[l, q] * inv[j]
                z[l] = z[l] - m[l][j] * z[j]
                if ahead:
                    ahead[l] = ahead[l] - m[l][j] * ahead[j]
            if ahead:
                following = following - (ahead[j] * inv[j]) * z[j]
        w = z[0] * lax.rsqrt(a[0][0])
        for i in range(1, 8):
            w = jnp.where(sub == i, z[i] * lax.rsqrt(a[i][i]), w)
        out.append(jnp.where(lane < k0 + 8, w, 0.0))
        if p == 15:
            break
        y = [z[j] * inv[j] for j in range(8)]
        for l in range(7, 0, -1):
            for j in range(l):
                y[j] = y[j] - m[l][j] * y[l]
        rows[p + 1] = following
        for i in range(p + 2, 16):
            c = [jnp.broadcast_to(rows[i][:, k0 + j : k0 + j + 1], (8, 128)) for j in range(8)]
            t = [c[j] * y[j] for j in range(8)]
            t = ((t[0] + t[1]) + (t[2] + t[3])) + ((t[4] + t[5]) + (t[6] + t[7]))
            rows[i] = jnp.where(inside, 0.0, rows[i]) - t
    return out


def gram_kernel(*refs):
    part_refs, field_ref, tiles_ref = refs[:-2], refs[-2], refs[-1]
    rows = part_refs[0].shape[0] // BANDS
    for band in range(BANDS):
        for part, part_ref in enumerate(part_refs):
            at = (band * len(part_refs) + part) * rows
            field_ref[at : at + rows, :] = part_ref[band * rows : band * rows + rows, :]
    tile = 0
    for i in range(field_ref.shape[0] // 128):
        terms = lax.dot_general(
            field_ref[128 * i : 128 * i + 128, :],
            field_ref[: 128 * i + 128, :],
            (((1,), (1,)), ((), ())),
            preferred_element_type=jnp.float32,
        )
        for j in range(i + 1):
            tiles_ref[128 * tile : 128 * tile + 128, :] = terms[:, 128 * j : 128 * j + 128]
            tile += 1


def field_and_tiles(parts):
    rows = sum(part.shape[0] for part in parts)
    count = rows // 128
    return pl.pallas_call(
        gram_kernel,
        out_shape=[
            jax.ShapeDtypeStruct((rows, parts[0].shape[1]), jnp.bfloat16),
            jax.ShapeDtypeStruct((64 * count * (count + 1), 128), jnp.float32),
        ],
        in_specs=[pl.BlockSpec(memory_space=pltpu.VMEM)] * len(parts),
        out_specs=[pl.BlockSpec(memory_space=pltpu.VMEM)] * 2,
        compiler_params=pltpu.CompilerParams(vmem_limit_bytes=32 * 1024 * 1024),
    )(*parts)


def rotation_kernel(tiles_ref, field_ref, out_ref, s_ref, a_ref, w_ref, r_ref):
    n, b = field_ref.shape[0], 128
    tile = 0
    for i in range(n // b):
        for j in range(i + 1):
            s_ref[b * i : b * i + b, b * j : b * j + b] = tiles_ref[b * tile : b * tile + b, :]
            tile += 1
    for k in range(n // b):
        lo, hi = k * b, (k + 1) * b
        out = inverse_factor_of_block([s_ref[lo + 8 * i : lo + 8 * i + 8, lo:hi] for i in range(16)])
        for i in range(16):
            w_ref[8 * i : 8 * i + 8, :] = out[i]
        w = w_ref[...]
        r_ref[lo:hi, lo:hi] = w.astype(jnp.bfloat16)
        if hi < n:
            lower = dot_nt(s_ref[hi:, lo:hi], w)
            s_ref[hi:, hi:] -= dot_nt(lower, lower)
        if k > 0:
            v = dot_nn(w, a_ref[lo:hi, :lo])
            r_ref[lo:hi, :lo] = v.astype(jnp.bfloat16)
            if hi < n:
                a_ref[hi:, :lo] -= dot_nn(lower, v)
        if hi < n:
            a_ref[hi:, lo:hi] = -dot_nn(lower, w)
        turned = jnp.dot(r_ref[lo:hi, :hi], field_ref[:hi, :], preferred_element_type=jnp.float32)
        out_ref[lo:hi, :] = turned.astype(jnp.bfloat16)


def rotated_by(tiles, field):
    n = field.shape[0]
    return pl.pallas_call(
        rotation_kernel,
        out_shape=jax.ShapeDtypeStruct(field.shape, jnp.bfloat16),
        in_specs=[pl.BlockSpec(memory_space=pltpu.VMEM)] * 2,
        out_specs=pl.BlockSpec(memory_space=pltpu.VMEM),
        scratch_shapes=[
            pltpu.VMEM((n, n), jnp.float32),
            pltpu.VMEM((n, n), jnp.float32),
            pltpu.VMEM((128, 128), jnp.float32),
            pltpu.VMEM((n, n), jnp.bfloat16),
        ],
        compiler_params=pltpu.CompilerParams(vmem_limit_bytes=32 * 1024 * 1024),
    )(tiles, field)


def exchange(pieces, axis):
    return lax.all_to_all(pieces, axis, 0, 0, tiled=True)


def summed_everywhere(terms, scale):
    near, far = lax.axis_size(NEAR), lax.axis_size("z")
    rows = terms.shape[0] // near
    part = jnp.sum(exchange(terms.reshape(near, rows, 128), NEAR), axis=0)
    part = jnp.sum(exchange(part.reshape(far, rows // far, 128), "z"), axis=0)
    part = (part + lax.ppermute(part, "x_hi", [(0, 1), (1, 0)])) * scale
    part = exchange(jnp.broadcast_to(part[None], (far,) + part.shape), "z").reshape(rows, 128)
    bands = lax.axis_size(BAND)
    part = exchange(jnp.broadcast_to(part[None], (bands, rows, 128)), BAND).reshape(-1, 128)
    return lax.all_gather(part, "core", axis=0, tiled=True)


def local(orbitals, potential):
    cells_dev = orbitals.shape[1] * orbitals.shape[2] * orbitals.shape[3]
    total_cells = cells_dev * lax.axis_size(DOM)
    slabs = orbitals.reshape(PARTS, -1, orbitals.shape[3])
    filtered = chebyshev([slabs[g] for g in range(PARTS)], potential.reshape(-1, potential.shape[2]))
    shares = [
        lax.all_to_all(part.reshape(-1, cells_dev), BAND, 1, 0, tiled=True) for part in filtered
    ]
    everyone, terms = field_and_tiles(shares)
    tiles = summed_everywhere(terms, 1.0 / total_cells)
    turned = rotated_by(tiles, everyone)
    result = lax.all_to_all(turned, BAND, 0, 1, tiled=True)
    return result.reshape(orbitals.shape)


def solution(mesh):
    named = Mesh(mesh.devices.reshape(4, 2, 2, 16, 2), ("y", "x_lo", "x_hi", "z", "core"))
    placed = (P(BAND, DOM, None, None), P(DOM, None, None))
    return jax.shard_map(
        local, mesh=named, in_specs=placed, out_specs=P(BAND, DOM, None, None), check_vma=False
    )
```

```python
from functools import partial

import jax
import jax.numpy as jnp
import numpy as np
from jax import lax
from jax.experimental import pallas as pl
from jax.experimental.pallas import tpu as pltpu
from jax.sharding import Mesh
from jax.sharding import PartitionSpec as P

BAND, DOM = ("y", "x_lo"), ("x_hi", "z", "core")
NEAR = ("core", "y", "x_lo")

BANDS, PARTS = 8, 2

HIGHEST = lax.Precision.HIGHEST

spectrum_center = 7.5
spectrum_half = 4.5


def stencil_matrices():
    def band(count):
        away = np.abs(np.arange(count)[:, None] - np.arange(count)[None, :])
        return 16.0 * (away == 1) - 1.0 * (away == 2)

    eye, none = np.eye(32), np.zeros((32, 32))
    own = np.block([[band(32), 16.0 * eye], [16.0 * eye, band(32)]])
    left = np.block([[-eye, 16.0 * eye], [none, -eye]])
    right = np.block([[-eye, none], [16.0 * eye, -eye]])
    across = [np.kron(np.eye(2), part) for part in (left, own, right)]
    return np.concatenate(across, axis=1), band(128) - 90.0 * np.eye(128)


def stencil_kernel(degree, left_ref, cells_ref, right_ref, potential_ref, across_ref, along_ref, *rest):
    out_ref = rest[-1]
    double = 1.0 if degree == 0 else 2.0
    weight = (potential_ref[...] - spectrum_center) * (double / spectrum_half)
    weight = jnp.concatenate([weight, weight], axis=0)
    for step in range(cells_ref.shape[0] // 128):
        rows = slice(128 * step, 128 * step + 128)
        cells = cells_ref[rows, :]
        stack = jnp.concatenate([left_ref[rows, :], cells, right_ref[rows, :]], axis=0)
        laplace = jnp.dot(across_ref[...], stack, preferred_element_type=jnp.float32)
        laplace += jnp.dot(cells, along_ref[...], preferred_element_type=jnp.float32)
        image = weight * cells.astype(jnp.float32) - laplace * (double / (24.0 * spectrum_half))
        if degree > 0:
            image = image - rest[0][rows, :].astype(jnp.float32)
        out_ref[rows, :] = image.astype(jnp.bfloat16)


def filtered_by_one(degree, sides, cells, before, potential, matrices):
    operands = [sides[0], cells, sides[1], potential, *matrices] + ([before] if degree > 0 else [])
    return pl.pallas_call(
        partial(stencil_kernel, degree),
        out_shape=jax.ShapeDtypeStruct(cells.shape, jnp.bfloat16),
        in_specs=[pl.BlockSpec(memory_space=pltpu.VMEM)] * len(operands),
        out_specs=pl.BlockSpec(memory_space=pltpu.VMEM),
        compiler_params=pltpu.CompilerParams(vmem_limit_bytes=32 * 1024 * 1024),
        cost_estimate=pl.CostEstimate(
            flops=1024 * cells.size, bytes_accessed=10 * cells.size, transcendentals=0
        ),
    )(*operands)


def halo(cells):
    count = lax.axis_size(DOM)
    left = lax.ppermute(cells, DOM, [(i, i + 1) for i in range(count - 1)])
    right = lax.ppermute(cells, DOM, [(i + 1, i) for i in range(count - 1)])
    return left, right


def chebyshev(groups, potential):
    matrices = [jnp.asarray(part, jnp.bfloat16) for part in stencil_matrices()]
    latest, previous = list(groups), [None] * len(groups)
    sides = [halo(cells) for cells in latest]
    for degree in range(3):
        for g in range(len(groups)):
            cells = latest[g]
            latest[g] = filtered_by_one(degree, sides[g], cells, previous[g], potential, matrices)
            previous[g] = cells
            if degree < 2:
                sides[g] = halo(latest[g])
    return latest


def dot_nn(a, b):
    return lax.dot_general(a, b, (((1,), (0,)), ((), ())), precision=HIGHEST, preferred_element_type=jnp.float32)


def dot_nt(a, b):
    return lax.dot_general(a, b, (((1,), (1,)), ((), ())), precision=HIGHEST, preferred_element_type=jnp.float32)


def inverse_factor_of_block(rows):
    lane = lax.broadcasted_iota(jnp.int32, (8, 128), 1)
    sub = lax.broadcasted_iota(jnp.int32, (8, 128), 0)
    rows = list(rows)
    out = []
    for p in range(16):
        k0 = 8 * p
        inside = (lane >= k0) & (lane < k0 + 8)
        x = rows[p]
        columns = [jnp.broadcast_to(x[:, k0 + j : k0 + j + 1], (8, 128)) for j in range(8)]
        a = [[jnp.broadcast_to(columns[j][i : i + 1, :], (8, 128)) for j in range(i + 1)] for i in range(8)]
        x = jnp.where(inside, (lane - k0 == sub).astype(jnp.float32), x)
        z = [jnp.broadcast_to(x[i : i + 1, :], (8, 128)) for i in range(8)]
        inv, m = [], [[None] * 8 for _ in range(8)]
        ahead = []
        if p < 15:
            ahead = [jnp.broadcast_to(rows[p + 1][:, k0 + j : k0 + j + 1], (8, 128)) for j in range(8)]
            following = jnp.where(inside, 0.0, rows[p + 1])
        for j in range(8):
            products = {(l, q): a[l][j] * a[q][j] for l in range(j + 1, 8) for q in range(j + 1, l + 1)}
            inv.append(1.0 / a[j][j])
            for l in range(j + 1, 8):
                m[l][j] = a[l][j] * inv[j]
                for q in range(j + 1, l + 1):
                    a[l][q] = a[l][q] - products[l, q] * inv[j]
                z[l] = z[l] - m[l][j] * z[j]
                if ahead:
                    ahead[l] = ahead[l] - m[l][j] * ahead[j]
            if ahead:
                following = following - (ahead[j] * inv[j]) * z[j]
        w = z[0] * lax.rsqrt(a[0][0])
        for i in range(1, 8):
            w = jnp.where(sub == i, z[i] * lax.rsqrt(a[i][i]), w)
        out.append(jnp.where(lane < k0 + 8, w, 0.0))
        if p == 15:
            break
        y = [z[j] * inv[j] for j in range(8)]
        for l in range(7, 0, -1):
            for j in range(l):
                y[j] = y[j] - m[l][j] * y[l]
        rows[p + 1] = following
        for i in range(p + 2, 16):
            c = [jnp.broadcast_to(rows[i][:, k0 + j : k0 + j + 1], (8, 128)) for j in range(8)]
            t = [c[j] * y[j] for j in range(8)]
            t = ((t[0] + t[1]) + (t[2] + t[3])) + ((t[4] + t[5]) + (t[6] + t[7]))
            rows[i] = jnp.where(inside, 0.0, rows[i]) - t
    return out


def gram_kernel(*refs):
    part_refs, field_ref, tiles_ref = refs[:-2], refs[-2], refs[-1]
    rows = part_refs[0].shape[0] // BANDS
    for band in range(BANDS):
        for part, part_ref in enumerate(part_refs):
            at = (band * len(part_refs) + part) * rows
            field_ref[at : at + rows, :] = part_ref[band * rows : band * rows + rows, :]
    tile = 0
    for i in range(field_ref.shape[0] // 128):
        terms = lax.dot_general(
            field_ref[128 * i : 128 * i + 128, :],
            field_ref[: 128 * i + 128, :],
            (((1,), (1,)), ((), ())),
            preferred_element_type=jnp.float32,
        )
        for j in range(i + 1):
            tiles_ref[128 * tile : 128 * tile + 128, :] = terms[:, 128 * j : 128 * j + 128]
            tile += 1


def field_and_tiles(parts):
    rows = sum(part.shape[0] for part in parts)
    count = rows // 128
    return pl.pallas_call(
        gram_kernel,
        out_shape=[
            jax.ShapeDtypeStruct((rows, parts[0].shape[1]), jnp.bfloat16),
            jax.ShapeDtypeStruct((64 * count * (count + 1), 128), jnp.float32),
        ],
        in_specs=[pl.BlockSpec(memory_space=pltpu.VMEM)] * len(parts),
        out_specs=[pl.BlockSpec(memory_space=pltpu.VMEM)] * 2,
        compiler_params=pltpu.CompilerParams(vmem_limit_bytes=32 * 1024 * 1024),
    )(*parts)


def rotation_kernel(tiles_ref, field_ref, out_ref, s_ref, a_ref, w_ref, r_ref):
    n, b = field_ref.shape[0], 128
    tile = 0
    for i in range(n // b):
        for j in range(i + 1):
            s_ref[b * i : b * i + b, b * j : b * j + b] = tiles_ref[b * tile : b * tile + b, :]
            tile += 1
    for k in range(n // b):
        lo, hi = k * b, (k + 1) * b
        out = inverse_factor_of_block([s_ref[lo + 8 * i : lo + 8 * i + 8, lo:hi] for i in range(16)])
        for i in range(16):
            w_ref[8 * i : 8 * i + 8, :] = out[i]
        w = w_ref[...]
        r_ref[lo:hi, lo:hi] = w.astype(jnp.bfloat16)
        if hi < n:
            lower = dot_nt(s_ref[hi:, lo:hi], w)
            s_ref[hi:, hi:] -= dot_nt(lower, lower)
        if k > 0:
            v = dot_nn(w, a_ref[lo:hi, :lo])
            r_ref[lo:hi, :lo] = v.astype(jnp.bfloat16)
            if hi < n:
                a_ref[hi:, :lo] -= dot_nn(lower, v)
        if hi < n:
            a_ref[hi:, lo:hi] = -dot_nn(lower, w)
        turned = jnp.dot(r_ref[lo:hi, :hi], field_ref[:hi, :], preferred_element_type=jnp.float32)
        out_ref[lo:hi, :] = turned.astype(jnp.bfloat16)


def rotated_by(tiles, field):
    n = field.shape[0]
    return pl.pallas_call(
        rotation_kernel,
        out_shape=jax.ShapeDtypeStruct(field.shape, jnp.bfloat16),
        in_specs=[pl.BlockSpec(memory_space=pltpu.VMEM)] * 2,
        out_specs=pl.BlockSpec(memory_space=pltpu.VMEM),
        scratch_shapes=[
            pltpu.VMEM((n, n), jnp.float32),
            pltpu.VMEM((n, n), jnp.float32),
            pltpu.VMEM((128, 128), jnp.float32),
            pltpu.VMEM((n, n), jnp.bfloat16),
        ],
        compiler_params=pltpu.CompilerParams(vmem_limit_bytes=32 * 1024 * 1024),
    )(tiles, field)


def exchange(pieces, axis):
    return lax.all_to_all(pieces, axis, 0, 0, tiled=True)


def summed_everywhere(terms, scale):
    near, far = lax.axis_size(NEAR), lax.axis_size("z")
    rows = terms.shape[0] // near
    part = jnp.sum(exchange(terms.reshape(near, rows, 128), NEAR), axis=0)
    part = jnp.sum(exchange(part.reshape(far, rows // far, 128), "z"), axis=0)
    part = (part + lax.ppermute(part, "x_hi", [(0, 1), (1, 0)])) * scale
    part = exchange(jnp.broadcast_to(part[None], (far,) + part.shape), "z").reshape(rows, 128)
    bands = lax.axis_size(BAND)
    part = exchange(jnp.broadcast_to(part[None], (bands, rows, 128)), BAND).reshape(-1, 128)
    return lax.all_gather(part, "core", axis=0, tiled=True)


def local(orbitals, potential):
    cells_dev = orbitals.shape[1] * orbitals.shape[2] * orbitals.shape[3]
    total_cells = cells_dev * lax.axis_size(DOM)
    slabs = orbitals.reshape(PARTS, -1, orbitals.shape[3])
    parts = [slabs[0]]
    for g in range(1, PARTS):
        slabs, parts[-1] = lax.optimization_barrier((slabs, parts[-1]))
        parts.append(slabs[g])
    filtered = chebyshev(parts, potential.reshape(-1, potential.shape[2]))
    shares = [
        lax.all_to_all(part.reshape(-1, cells_dev), BAND, 1, 0, tiled=True) for part in filtered
    ]
    everyone, terms = field_and_tiles(shares)
    tiles = summed_everywhere(terms, 1.0 / total_cells)
    turned = rotated_by(tiles, everyone)
    result = lax.all_to_all(turned, BAND, 0, 1, tiled=True)
    return result.reshape(orbitals.shape)


def solution(mesh):
    named = Mesh(mesh.devices.reshape(4, 2, 2, 16, 2), ("y", "x_lo", "x_hi", "z", "core"))
    placed = (P(BAND, DOM, None, None), P(DOM, None, None))
    return jax.shard_map(
        local, mesh=named, in_specs=placed, out_specs=P(BAND, DOM, None, None), check_vma=False
    )
```
